32 devices in a mesh: ctx: 16 (over z, y, x), tp: 2 (over core).
Axes of the slice: x: 2, y: 2, z: 4, core: 2. Of those that a mesh axis runs over, the one named last changes fastest.
Arguments:
- lin_query: bfloat16 [2048, 4096], P('ctx', 'tp'), may hold values from -6 to 6
- lin_key: bfloat16 [2048, 4096], P('ctx', 'tp'), may hold values from -6 to 6
- lin_value: bfloat16 [2048, 4096], P('ctx', 'tp'), may hold values from -6 to 6
- lin_cotangent: bfloat16 [2048, 4096], P('ctx', 'tp'), may hold values from -6 to 6
- soft_query: bfloat16 [2048, 4096], P('ctx', 'tp'), may hold values from -200 to 200
- soft_key: bfloat16 [2048, 1024], P('ctx', 'tp'), may hold values from -200 to 200
- soft_value: bfloat16 [2048, 1024], P('ctx', 'tp'), may hold values from -6 to 6
- doc_start: int32 [2048], P('ctx'), may hold values from 0 to 2047, as said below
Outputs:
- lin_out: bfloat16 [2048, 4096], P('ctx', 'tp')
- grad_query: bfloat16 [2048, 4096], P('ctx', 'tp')
- grad_key: bfloat16 [2048, 4096], P('ctx', 'tp')
- grad_value: bfloat16 [2048, 4096], P('ctx', 'tp')
- soft_out: bfloat16 [2048, 4096], P('ctx', 'tp')
The draws below stay inside these ranges and needn't reach their ends.
Inputs may be any that keep to these rules, and one draw needn't show every extreme that they name: doc_start[i] <= i, doc_start never falls along the sequence, doc_start[0] = 0, doc_start[i] equals i or doc_start[i - 1], and a document of one position starts at position 2047.
All inputs are finite; a program needn't handle non-finite values.
Results may differ from the reference program's by a relative error of at most 0.011.
Values may be sent and summed in bfloat16 or wider, within the bound.
A program may use at most 128 MiB of HBM per device.

```python
import math
import jax
import jax.numpy as jnp
from jax import lax

HD = 128
LH = 32
SH = 32
KVH = 8
T_DEV = 128
SEQ = 2048
DOC_MEAN = 512
N_CTX = 16


def paired_draw(key):
    query_key, key_key = jax.random.split(jax.random.fold_in(key, 17), 2)
    queries = jax.random.normal(query_key, (SEQ, SH, HD), jnp.float32)
    keys = jax.random.normal(key_key, (SEQ, KVH, HD), jnp.float32)
    return (queries.reshape(SEQ, SH * HD), keys.reshape(SEQ, KVH * HD))


def draw_soft_query(key, part):
    return paired_draw(key)[0].astype(jnp.bfloat16)


def draw_soft_key(key, part):
    return paired_draw(key)[1].astype(jnp.bfloat16)


def draw_doc_start(key, part):
    marks = jax.random.randint(jax.random.fold_in(key, 5), (SEQ,), 0, DOC_MEAN)
    positions = jnp.arange(SEQ, dtype=jnp.int32)
    quiet = (positions > SEQ // 4) & (positions < 3 * SEQ // 4 + T_DEV)
    opens = (marks == 0) & jnp.logical_not(quiet) | (positions == 0) | (positions == SEQ - 1)
    begins = jnp.where(opens, positions, 0).astype(jnp.int32)
    return lax.cummax(begins, axis=0)


def shard_levels(own_key, shape, cuts, least, largest):
    level, own = 1.0, jax.random.fold_in(own_key, 6)
    for axis_at, blocks in cuts:
        steps = jnp.exp(jax.random.uniform(jax.random.fold_in(own, axis_at), (blocks,), jnp.float32, least / len(cuts), largest / len(cuts)))
        level = level * jnp.repeat(steps, shape[axis_at] // blocks).reshape([-1 if axis == axis_at else 1 for axis in range(len(shape))])
    return level


def normal_values(stream_key, extent, width, limit, shards=(), held_as=jnp.bfloat16):
    values = width * jax.random.normal(stream_key, extent, jnp.float32)
    if shards:
        values = values * shard_levels(stream_key, extent, shards, -0.22, 0.18)
    return jnp.clip(values, -limit, limit).astype(held_as)


def setup_inputs(seed: int = 0) -> dict:
    arg_keys = jax.random.split(jax.random.key(seed), 9)
    lin_query = normal_values(arg_keys[0], (SEQ, LH * HD), 1.0, 6.0, ((0, 16), (1, 2)))
    lin_key = normal_values(arg_keys[1], (SEQ, LH * HD), 1.0, 6.0, ((0, 16), (1, 2)))
    lin_value = normal_values(arg_keys[2], (SEQ, LH * HD), 1.0, 6.0, ((0, 16), (1, 2)))
    lin_cotangent = normal_values(arg_keys[3], (SEQ, LH * HD), 1.0, 6.0, ((0, 16), (1, 2)))
    soft_query = draw_soft_query(jax.random.fold_in(arg_keys[8], 71), 0)
    soft_key = draw_soft_key(jax.random.fold_in(arg_keys[8], 71), 0)
    soft_value = normal_values(arg_keys[6], (SEQ, KVH * HD), 1.0, 6.0, ((0, 16), (1, 2)))
    doc_start = draw_doc_start(jax.random.fold_in(arg_keys[8], 71), 0)
    return {"lin_query": lin_query, "lin_key": lin_key, "lin_value": lin_value, "lin_cotangent": lin_cotangent, "soft_query": soft_query, "soft_key": soft_key, "soft_value": soft_value, "doc_start": doc_start}


epsilon = 1e-06
highest = lax.Precision.HIGHEST
floor_score = -1e+30

def rounded(value):
    return lax.optimization_barrier(value.astype(jnp.bfloat16)).astype(jnp.float32)

def causal_scores(left, right, lower):
    raw = jnp.einsum('thd,shd->hts', left, right, precision=highest)
    return rounded(jnp.where(lower[None], raw, 0.0))

def outer_sum(left, right):
    return jnp.einsum('thd,the->hde', left, right, precision=highest)

def lightning(lin_query, lin_key, lin_value, lin_cotangent):
    shape = (N_CTX, T_DEV, LH, HD)
    queries = lin_query.astype(jnp.float32).reshape(shape)
    keys = lin_key.astype(jnp.float32).reshape(shape)
    values = lin_value.astype(jnp.float32).reshape(shape)
    lower = jnp.tril(jnp.ones((T_DEV, T_DEV), dtype=bool))
    zero_state = jnp.zeros((LH, HD, HD), jnp.float32)

    def forward(state, item):
        query_block, key_block, value_block = item
        weights = causal_scores(query_block, key_block, lower)
        mixed = jnp.einsum('hts,shd->thd', weights, value_block, precision=highest)
        mixed = mixed + jnp.einsum('thd,hde->the', query_block, state, precision=highest)
        return (state + outer_sum(key_block, value_block), mixed)
    unused, mixed = lax.scan(forward, zero_state, (queries, keys, values))
    mixed = mixed.reshape(SEQ, LH * HD)
    scale = lax.rsqrt(lax.optimization_barrier(jnp.mean(mixed * mixed, axis=1)) + epsilon)
    normed = mixed * scale[:, None]
    lin_out = normed.astype(jnp.bfloat16)
    grad = lin_cotangent.astype(jnp.float32)
    inner = lax.optimization_barrier(jnp.mean(grad * normed, axis=1))
    grad_mix = rounded(scale[:, None] * (grad - normed * inner[:, None])).reshape(shape)

    def query_pass(state, item):
        key_block, value_block, grad_block = item
        grad_scores = causal_scores(grad_block, value_block, lower)
        grad_q = jnp.einsum('hts,shd->thd', grad_scores, key_block, precision=highest)
        grad_q = grad_q + jnp.einsum('the,hde->thd', grad_block, state, precision=highest)
        return (state + outer_sum(key_block, value_block), grad_q)
    unused, grad_q = lax.scan(query_pass, zero_state, (keys, values, grad_mix))

    def key_pass(state, item):
        query_block, key_block, value_block, grad_block = item
        weights = causal_scores(query_block, key_block, lower)
        grad_scores = causal_scores(grad_block, value_block, lower)
        grad_k = jnp.einsum('hts,thd->shd', grad_scores, query_block, precision=highest)
        grad_k = grad_k + jnp.einsum('she,hde->shd', value_block, state, precision=highest)
        grad_v = jnp.einsum('hts,thd->shd', weights, grad_block, precision=highest)
        grad_v = grad_v + jnp.einsum('shd,hde->she', key_block, state, precision=highest)
        return (state + outer_sum(query_block, grad_block), (grad_k, grad_v))
    unused, (grad_k, grad_v) = lax.scan(key_pass, zero_state, (queries, keys, values, grad_mix), reverse=True)
    grad_query = grad_q.reshape(SEQ, LH * HD).astype(jnp.bfloat16)
    grad_key = grad_k.reshape(SEQ, LH * HD).astype(jnp.bfloat16)
    grad_value = grad_v.reshape(SEQ, LH * HD).astype(jnp.bfloat16)
    return (lin_out, grad_query, grad_key, grad_value)

def softmax_layer(soft_query, soft_key, soft_value, doc_start):
    group = SH // KVH
    scale = 1.0 / math.sqrt(HD)
    queries = soft_query.astype(jnp.float32).reshape(N_CTX, T_DEV, KVH, group, HD)
    starts = doc_start.reshape(N_CTX, T_DEV)
    keys = soft_key.astype(jnp.float32).reshape(SEQ, KVH, HD)
    values = soft_value.astype(jnp.float32).reshape(SEQ, KVH, HD)
    key_pos = jnp.arange(SEQ, dtype=jnp.int32)
    blocks = jnp.arange(N_CTX, dtype=jnp.int32)

    def one_block(item):
        query_block, start_block, index = item
        query_pos = index * T_DEV + jnp.arange(T_DEV, dtype=jnp.int32)
        allowed = (key_pos[None, :] <= query_pos[:, None]) & (key_pos[None, :] >= start_block[:, None])
        scores = jnp.einsum('tkgd,nkd->kgtn', query_block, keys, precision=highest) * scale
        scores = jnp.where(allowed, scores, floor_score)
        top = lax.optimization_barrier(jnp.max(scores, axis=-1))
        weights = jnp.where(allowed, jnp.exp(scores - top[..., None]), 0.0)
        total = lax.optimization_barrier(jnp.sum(weights, axis=-1))
        mixed = jnp.einsum('kgtn,nkd->kgtd', rounded(weights), values, precision=highest)
        out = mixed / total[..., None]
        return jnp.transpose(out, (2, 0, 1, 3)).reshape(T_DEV, SH * HD).astype(jnp.bfloat16)
    result = lax.map(one_block, (queries, starts, blocks))
    return result.reshape(SEQ, SH * HD)

def reference(lin_query, lin_key, lin_value, lin_cotangent, soft_query, soft_key, soft_value, doc_start):
    lin_out, grad_query, grad_key, grad_value = lightning(lin_query, lin_key, lin_value, lin_cotangent)
    soft_out = softmax_layer(soft_query, soft_key, soft_value, doc_start)
    return (lin_out, grad_query, grad_key, grad_value, soft_out)
```

```python
import functools
import math

import jax
import jax.numpy as jnp
from jax import lax
from jax.experimental import pallas as pl
from jax.experimental.pallas import tpu as pltpu
from jax.sharding import PartitionSpec as P

HD = 128
G = 4

MESH = pl.DeviceIdType.MESH
epsilon = 1e-06
floor_score = -1e30
f32 = jnp.float32
bf16 = jnp.bfloat16


def dot(a, b, ca, cb):
    return lax.dot_general(a, b, (((ca,), (cb,)), ((), ())), preferred_element_type=f32)


def kernel(
    n,
    n_tp,
    lq, lk, lv, lg, sq, sk, sv, doc,
    lin_out, grad_q, grad_k, grad_v, soft_out,
    st_own, st_in, st_tot, st_z, st_out, st_fin,
    scores, mix, gmix, gk_acc, gv_acc,
    ex_own, ex_in,
    kv, q_in, q_rows, doc_in, o_own, top, total, acc,
    a_send, a_recv, z_send, z_recv, c_send, c_recv,
    e_send, e_recv, s_send, s_recv, kvz_send, kvz_recv, o_send, o_recv,
):
    length = lq.shape[0]
    heads = lq.shape[1] // HD
    hq = heads // G
    planes = n // G
    q_heads = sq.shape[1] // HD
    kv_heads = sk.shape[1] // HD
    mine = q_heads // G
    qw = mine * HD
    unit = min(4, heads)
    me = lax.axis_index("ctx")
    tp = lax.axis_index("tp")
    z = me // G
    p = lax.rem(me, G)

    def member(d):
        return lax.rem(p + d, G)

    def at_member(r):
        return {"ctx": z * G + r}

    def at_plane(zz):
        return {"ctx": zz * G + p}

    def remote(src, dst, send, recv, device):
        return pltpu.make_async_remote_copy(
            src_ref=src, dst_ref=dst, send_sem=send, recv_sem=recv,
            device_id=device, device_id_type=MESH,
        )

    barrier = pltpu.get_barrier_semaphore()
    for d in range(1, G):
        pl.semaphore_signal(barrier, inc=1, device_id=at_member(member(d)), device_id_type=MESH)
    for k in range(1, planes):
        pl.semaphore_signal(
            barrier, inc=1, device_id=at_plane(lax.rem(z + k, planes)), device_id_type=MESH
        )
    for k in range(1, n_tp):
        pl.semaphore_signal(
            barrier, inc=1, device_id={"tp": lax.rem(tp + k, n_tp)}, device_id_type=MESH
        )

    def lanes(h):
        return pl.ds(pl.multiple_of(h * HD, HD), HD)

    def per_heads(body):
        def step(i, _):
            body([i * unit + u for u in range(unit)])
            return 0

        lax.fori_loop(0, heads // unit, step, 0)

    def outer_states(way, left, right):
        def body(hs):
            ls = [left[:, lanes(h)] for h in hs]
            rs = [right[:, lanes(h)] for h in hs]
            out = [dot(a, b, 0, 0).astype(bf16) for a, b in zip(ls, rs)]
            for h, o in zip(hs, out):
                st_own[way, h] = o

        per_heads(body)

    outer_states(0, lk, lv)
    pl.semaphore_wait(barrier, (G - 1) + (planes - 1) + (n_tp - 1))

    def scan_a(way):
        return [
            remote(
                st_own.at[way, pl.ds(member(d) * hq, hq)], st_in.at[way, p],
                a_send.at[way, d - 1], a_recv.at[way, d - 1], at_member(member(d)),
            )
            for d in range(1, G)
        ]

    def scan_z(way, k):
        there = z - k if way else z + k
        return remote(
            st_tot.at[way], st_z.at[way, k - 1],
            z_send.at[way, k - 1], z_recv.at[way, k - 1], at_plane(there),
        )

    def sends_z(way, k):
        return (z - k >= 0) if way else (z + k < planes)

    def scan_c(way):
        return [
            remote(
                st_out.at[way, member(d)], st_fin.at[way, pl.ds(p * hq, hq)],
                c_send.at[way, d - 1], c_recv.at[way, d - 1], at_member(member(d)),
            )
            for d in range(1, G)
        ]

    def scan_start(way):
        for copy in scan_a(way):
            copy.start()
        st_in[way, p] = st_own[way, pl.ds(p * hq, hq)]

    def scan_middle(way):
        for copy in scan_a(way):
            copy.wait_recv()
        for h in range(hq):
            parts = [st_in[way, s, h].astype(f32) for s in range(G)]
            st_tot[way, h] = ((parts[0] + parts[1]) + (parts[2] + parts[3])).astype(bf16)
        for k in range(1, planes):

            @pl.when(sends_z(way, k))
            def _():
                scan_z(way, k).start()

    def scan_end(way):
        for k in range(1, planes):

            @pl.when(sends_z(1 - way, k))
            def _():
                scan_z(way, k).wait_recv()

        for h in range(hq):
            carry = jnp.zeros((HD, HD), f32)
            for k in range(1, planes):
                here = jnp.where(sends_z(1 - way, k), 1.0, 0.0)
                got = st_z[way, k - 1, h].astype(f32)
                carry = carry + jnp.where(here > 0.5, got, 0.0)
            order = range(G - 1, -1, -1) if way else range(G)
            for s in order:
                st_out[way, s, h] = carry.astype(bf16)
                carry = carry + st_in[way, s, h].astype(f32)
        for copy in scan_c(way):
            copy.start()
        st_fin[way, pl.ds(p * hq, hq)] = st_out[way, p]

    def scan_done(way):
        for copy in scan_c(way):
            copy.wait_recv()

    scan_start(0)

    def kv_lanes(r):
        return pl.ds(pl.multiple_of((r * kv_heads // G) * HD, HD), HD)

    def soft_copies():
        out = []
        for d in range(1, G):
            r = member(d)
            rows = pl.ds(p * length, length)
            for i, (src, dst) in enumerate(
                (
                    (sk.at[:, kv_lanes(r)], kv.at[z, 0, rows]),
                    (sv.at[:, kv_lanes(r)], kv.at[z, 1, rows]),
                    (doc, doc_in.at[p]),
                    (sq.at[:, pl.ds(pl.multiple_of(r * qw, HD), qw)], q_in.at[p]),
                )
            ):
                out.append(
                    remote(src, dst, s_send.at[d - 1, i], s_recv.at[d - 1, i], at_member(r))
                )
        return out

    for copy in soft_copies():
        copy.start()
    own_rows = pl.ds(pl.multiple_of(p * length, length), length)
    kv[z, 0, own_rows] = sk[:, kv_lanes(p)]
    kv[z, 1, own_rows] = sv[:, kv_lanes(p)]
    doc_in[p] = doc[...]
    q_in[p] = sq[:, pl.ds(pl.multiple_of(p * qw, HD), qw)]

    lower = lax.broadcasted_iota(jnp.int32, (length, length), 0) >= lax.broadcasted_iota(
        jnp.int32, (length, length), 1
    )

    def intra_forward(hs):
        qs = [lq[:, lanes(h)] for h in hs]
        ks = [lk[:, lanes(h)] for h in hs]
        vs = [lv[:, lanes(h)] for h in hs]
        ws = [jnp.where(lower, dot(a, b, 1, 1), 0.0).astype(bf16) for a, b in zip(qs, ks)]
        ms = [dot(w, v, 1, 0) for w, v in zip(ws, vs)]
        for h, w, m in zip(hs, ws, ms):
            scores[h] = w
            mix[:, lanes(h)] = m

    per_heads(intra_forward)
    scan_middle(0)

    for copy in soft_copies():
        copy.wait_recv()

    def kv_copy(k):
        return remote(
            kv.at[z], kv.at[z], kvz_send.at[k - 1], kvz_recv.at[k - 1], at_plane(z + k)
        )

    def kv_arrival(k):
        return remote(
            kv.at[z - k], kv.at[z - k], kvz_send.at[k - 1], kvz_recv.at[k - 1], at_plane(z - k)
        )

    for k in range(1, planes):

        @pl.when(z + k < planes)
        def _():
            kv_copy(k).start()

    span = G * length
    factor = math.log2(math.e) / math.sqrt(HD)

    def tile(b, zz, first):
        keys = kv[zz, 0]
        vals = kv[zz, 1]
        raw = dot(keys, q_rows[b], 1, 1) * factor
        key_pos = zz * span + lax.broadcasted_iota(jnp.int32, (span, qw), 0)
        begins = jnp.concatenate([doc_in[b][0:1, :]] * mine, axis=1)
        allowed = key_pos >= begins
        if first:
            one = lax.broadcasted_iota(jnp.int32, (1, length), 1)
            q_pos = z * span + b * length + jnp.concatenate([one] * mine, axis=1)
            allowed = allowed & (key_pos <= q_pos)
        raw = jnp.where(allowed, raw, floor_score)
        high = jnp.max(raw, axis=0, keepdims=True)
        if not first:
            old = top[b]
            high = jnp.maximum(old, high)
            shrink = jnp.exp2(old - high)
        probs = jnp.exp2(raw - high)
        summed = jnp.sum(probs, axis=0, keepdims=True)
        update = dot(vals, probs.astype(bf16), 0, 0)
        top[b] = high
        if first:
            total[b] = summed
            acc[b] = update
        else:
            total[b] = total[b] * shrink + summed
            acc[b] = acc[b] * shrink + update

    def own_tile(b, _):
        for h in range(mine):
            q_rows[b, h * length : (h + 1) * length, :] = q_in[b, :, h * HD : (h + 1) * HD]
        tile(b, z, True)
        return 0

    lax.fori_loop(0, G, own_tile, 0)
    scan_end(0)
    scan_done(0)

    ex_own[...] = jnp.zeros_like(ex_own)

    def inter_forward(hs):
        qs = [lq[:, lanes(h)] for h in hs]
        ss = [st_fin[0, h] for h in hs]
        ms = [mix[:, lanes(h)] + dot(a, s, 1, 0) for h, a, s in zip(hs, qs, ss)]
        gs = [lg[:, lanes(h)].astype(f32) for h in hs]
        square, inner = ex_own[0], ex_own[1]
        for m, g in zip(ms, gs):
            square = square + m * m
            inner = inner + g * m
        ex_own[0] = square
        ex_own[1] = inner
        for h, m in zip(hs, ms):
            mix[:, lanes(h)] = m

    per_heads(inter_forward)

    def exchange():
        return [
            remote(
                ex_own, ex_in.at[k - 1], e_send.at[k - 1], e_recv.at[k - 1],
                {"tp": lax.rem(tp + k, n_tp)},
            )
            for k in range(1, n_tp)
        ]

    for copy in exchange():
        copy.start()
    for copy in exchange():
        copy.wait_recv()
    square, inner = ex_own[0], ex_own[1]
    for k in range(n_tp - 1):
        square = square + ex_in[k, 0]
        inner = inner + ex_in[k, 1]
    features = heads * HD * n_tp
    scale = lax.rsqrt(jnp.sum(square, axis=1, keepdims=True) / features + epsilon)
    mean = scale * jnp.sum(inner, axis=1, keepdims=True) / features

    def turn(hs):
        qs = [lq[:, lanes(h)] for h in hs]
        ns = [mix[:, lanes(h)] * scale for h in hs]
        gs = [(scale * (lg[:, lanes(h)].astype(f32) - m * mean)).astype(bf16) for h, m in zip(hs, ns)]
        adj = [dot(a, g, 0, 0).astype(bf16) for a, g in zip(qs, gs)]
        for h, m, g, o in zip(hs, ns, gs, adj):
            lin_out[:, lanes(h)] = m.astype(bf16)
            gmix[:, lanes(h)] = g
            st_own[1, h] = o

    per_heads(turn)
    scan_start(1)

    def intra_backward(hs):
        qs = [lq[:, lanes(h)] for h in hs]
        ks = [lk[:, lanes(h)] for h in hs]
        vs = [lv[:, lanes(h)] for h in hs]
        gs = [gmix[:, lanes(h)] for h in hs]
        ss = [st_fin[0, h] for h in hs]
        ws = [scores[h] for h in hs]
        ds = [jnp.where(lower, dot(g, v, 1, 1), 0.0).astype(bf16) for g, v in zip(gs, vs)]
        gq = [dot(d, k, 1, 0) + dot(g, s, 1, 1) for d, k, g, s in zip(ds, ks, gs, ss)]
        gk = [dot(d, q, 0, 0) for d, q in zip(ds, qs)]
        gv = [dot(w, g, 0, 0) for w, g in zip(ws, gs)]
        for h, a, b, c in zip(hs, gq, gk, gv):
            grad_q[:, lanes(h)] = a.astype(bf16)
            gk_acc[:, lanes(h)] = b
            gv_acc[:, lanes(h)] = c

    per_heads(intra_backward)
    scan_middle(1)

    def earlier_plane(k, _):
        kv_arrival(k).wait_recv()

        def one(b, _):
            tile(b, z - k, False)
            return 0

        lax.fori_loop(0, G, one, 0)
        return 0

    lax.fori_loop(1, z + 1, earlier_plane, 0)
    scan_end(1)

    def finish(b, _):
        out = acc[b] / total[b]
        for h in range(mine):
            o_own[b, :, h * HD : (h + 1) * HD] = jnp.transpose(
                out[:, h * length : (h + 1) * length]
            ).astype(bf16)
        return 0

    lax.fori_loop(0, G, finish, 0)

    def out_copies():
        return [
            remote(
                o_own.at[member(d)], soft_out.at[:, pl.ds(pl.multiple_of(p * qw, HD), qw)],
                o_send.at[d - 1], o_recv.at[d - 1], at_member(member(d)),
            )
            for d in range(1, G)
        ]

    for copy in out_copies():
        copy.start()
    soft_out[:, pl.ds(pl.multiple_of(p * qw, HD), qw)] = o_own[p]
    scan_done(1)

    def inter_backward(hs):
        ks = [lk[:, lanes(h)] for h in hs]
        vs = [lv[:, lanes(h)] for h in hs]
        ss = [st_fin[1, h] for h in hs]
        gk = [gk_acc[:, lanes(h)] + dot(v, s, 1, 1) for h, v, s in zip(hs, vs, ss)]
        gv = [gv_acc[:, lanes(h)] + dot(k, s, 1, 0) for h, k, s in zip(hs, ks, ss)]
        for h, a, b in zip(hs, gk, gv):
            grad_k[:, lanes(h)] = a.astype(bf16)
            grad_v[:, lanes(h)] = b.astype(bf16)

    per_heads(inter_backward)

    for copy in out_copies():
        copy.wait_recv()
    for copy in scan_a(0) + scan_a(1) + scan_c(0) + scan_c(1):
        copy.wait_send()
    for copy in soft_copies() + exchange() + out_copies():
        copy.wait_send()
    for k in range(1, planes):

        @pl.when(z + k < planes)
        def _():
            kv_copy(k).wait_send()

        for way in (0, 1):

            @pl.when(sends_z(way, k))
            def _():
                scan_z(way, k).wait_send()


def on_device(n, n_tp, lq, lk, lv, lg, sq, sk, sv, doc_start):
    length, width = lq.shape
    heads = width // HD
    hq = heads // G
    planes = n // G
    q_width = sq.shape[1]
    qw = q_width // G
    doc = jnp.broadcast_to(doc_start[None, :], (8, length))
    dma = pltpu.SemaphoreType.DMA
    vm = pltpu.VMEM
    span = G * length
    others = planes - 1
    scratch = [
        vm((2, heads, HD, HD), bf16),
        vm((2, G, hq, HD, HD), bf16),
        vm((2, hq, HD, HD), bf16),
        vm((2, others, hq, HD, HD), bf16),
        vm((2, G, hq, HD, HD), bf16),
        vm((2, heads, HD, HD), bf16),
        vm((heads, length, length), bf16),
        vm((length, width), f32),
        vm((length, width), bf16),
        vm((length, width), f32),
        vm((length, width), f32),
        vm((2, length, HD), f32),
        vm((n_tp - 1, 2, length, HD), f32),
        vm((planes, 2, span, HD), bf16),
        vm((G, length, qw), bf16),
        vm((G, qw // HD * length, HD), bf16),
        vm((G, 8, length), jnp.int32),
        vm((G, length, qw), bf16),
        vm((G, 1, qw), f32),
        vm((G, 1, qw), f32),
        vm((G, HD, qw), f32),
        dma((2, G - 1)), dma((2, G - 1)),
        dma((2, others)), dma((2, others)),
        dma((2, G - 1)), dma((2, G - 1)),
        dma((n_tp - 1,)), dma((n_tp - 1,)),
        dma((G - 1, 4)), dma((G - 1, 4)),
        dma((others,)), dma((others,)),
        dma((G - 1,)), dma((G - 1,)),
    ]
    shape = jax.ShapeDtypeStruct((length, width), bf16)
    return pl.pallas_call(
        functools.partial(kernel, n, n_tp),
        out_shape=[shape] * 4 + [jax.ShapeDtypeStruct((length, q_width), bf16)],
        in_specs=[pl.BlockSpec(memory_space=pltpu.VMEM)] * 8,
        out_specs=[pl.BlockSpec(memory_space=pltpu.VMEM)] * 5,
        scratch_shapes=scratch,
        compiler_params=pltpu.CompilerParams(
            collective_id=0, has_side_effects=True, vmem_limit_bytes=48 * 1024 * 1024
        ),
    )(lq, lk, lv, lg, sq, sk, sv, doc)


def solution(mesh):
    wide = P("ctx", "tp")
    return jax.shard_map(
        functools.partial(on_device, mesh.shape["ctx"], mesh.shape["tp"]),
        mesh=mesh,
        in_specs=(wide,) * 7 + (P("ctx"),),
        out_specs=(wide,) * 5,
        check_vma=False,
    )
```

```python
import functools
import math

import jax
import jax.numpy as jnp
from jax import lax
from jax.experimental import pallas as pl
from jax.experimental.pallas import tpu as pltpu
from jax.sharding import PartitionSpec as P

HD = 128
G = 4

MESH = pl.DeviceIdType.MESH
epsilon = 1e-06
floor_score = -1e30
f32 = jnp.float32
bf16 = jnp.bfloat16


def dot(a, b, ca, cb):
    return lax.dot_general(a, b, (((ca,), (cb,)), ((), ())), preferred_element_type=f32)


def kernel(
    n,
    n_tp,
    lq_hbm, lk_hbm, lv_hbm, lg_hbm, sq_hbm, sk_hbm, sv_hbm, doc_row,
    lin_out, grad_q, grad_k, grad_v, soft_out,
    lq, lk, lv, lg, sq, sk, sv, doc, in_sems,
    st_own, st_in, st_tot, st_z, st_out, st_fin,
    scores, mix, gmix, gk_acc, gv_acc,
    ex_own, ex_in,
    kv, q_in, q_rows, doc_in, o_own, top, total, acc, carry_ref,
    a_send, a_recv, z_send, z_recv, c_send, c_recv,
    e_send, e_recv, s_send, s_recv, kvz_send, kvz_recv, o_send, o_recv,
):
    loads = [
        pltpu.make_async_copy(src, dst, in_sems.at[i])
        for i, (src, dst) in enumerate(
            (
                (lk_hbm, lk), (lv_hbm, lv), (lq_hbm, lq), (sk_hbm, sk),
                (sv_hbm, sv), (sq_hbm, sq), (lg_hbm, lg),
            )
        )
    ]
    for copy in loads:
        copy.start()
    length = lq.shape[0]
    heads = lq.shape[1] // HD
    hq = heads // G
    planes = n // G
    q_heads = sq.shape[1] // HD
    kv_heads = sk.shape[1] // HD
    mine = q_heads // G
    qw = mine * HD
    me = lax.axis_index("ctx")
    tp = lax.axis_index("tp")
    z = me // G
    p = lax.rem(me, G)

    def member(d):
        return lax.rem(p + d, G)

    def at_member(r):
        return {"ctx": z * G + r}

    def at_plane(zz):
        return {"ctx": zz * G + p}

    def remote(src, dst, send, recv, device):
        return pltpu.make_async_remote_copy(
            src_ref=src, dst_ref=dst, send_sem=send, recv_sem=recv,
            device_id=device, device_id_type=MESH,
        )

    barrier = pltpu.get_barrier_semaphore()
    for d in range(1, G):
        pl.semaphore_signal(barrier, inc=1, device_id=at_member(member(d)), device_id_type=MESH)
    for k in range(1, planes):
        pl.semaphore_signal(
            barrier, inc=1, device_id=at_plane(lax.rem(z + k, planes)), device_id_type=MESH
        )
    for k in range(1, n_tp):
        pl.semaphore_signal(
            barrier, inc=1, device_id={"tp": lax.rem(tp + k, n_tp)}, device_id_type=MESH
        )

    def lanes(h):
        return pl.ds(pl.multiple_of(h * HD, HD), HD)

    def chunk_heads(c):
        return [r * hq + c for r in range(G)]

    def per_chunk(body):
        for c in range(hq):
            body(chunk_heads(c))

    def per_chunk_loop(body):
        def step(c, _):
            body(chunk_heads(c))
            return 0

        lax.fori_loop(0, hq, step, 0)

    def scan_a(way, c):
        return [
            remote(
                st_own.at[way, member(d) * hq + c], st_in.at[way, p, c],
                a_send.at[way, d - 1, c], a_recv.at[way, d - 1, c], at_member(member(d)),
            )
            for d in range(1, G)
        ]

    def scan_z(way, k, c):
        there = z - k if way else z + k
        return remote(
            st_tot.at[way, c], st_z.at[way, k - 1, c],
            z_send.at[way, k - 1, c], z_recv.at[way, k - 1, c], at_plane(there),
        )

    def sends_z(way, k):
        return (z - k >= 0) if way else (z + k < planes)

    def scan_c(way, c):
        return [
            remote(
                st_out.at[way, member(d), c], st_fin.at[way, p * hq + c],
                c_send.at[way, d - 1, c], c_recv.at[way, d - 1, c], at_member(member(d)),
            )
            for d in range(1, G)
        ]

    def scan_start(way, c):
        for copy in scan_a(way, c):
            copy.start()
        st_in[way, p, c] = st_own[way, p * hq + c]

    def scan_middle(way, c):
        for copy in scan_a(way, c):
            copy.wait_recv()
        parts = [st_in[way, s, c].astype(f32) for s in range(G)]
        st_tot[way, c] = ((parts[0] + parts[1]) + (parts[2] + parts[3])).astype(bf16)
        for k in range(1, planes):

            @pl.when(sends_z(way, k))
            def _():
                scan_z(way, k, c).start()

    def scan_end(way, c):
        carry_ref[...] = jnp.zeros((HD, HD), f32)
        for k in range(1, planes):

            @pl.when(sends_z(1 - way, k))
            def _():
                scan_z(way, k, c).wait_recv()
                carry_ref[...] += st_z[way, k - 1, c].astype(f32)

        carry = carry_ref[...]
        order = range(G - 1, -1, -1) if way else range(G)
        for s in order:
            st_out[way, s, c] = carry.astype(bf16)
            carry = carry + st_in[way, s, c].astype(f32)
        for copy in scan_c(way, c):
            copy.start()
        st_fin[way, p * hq + c] = st_out[way, p, c]

    def scan_done(way, c):
        for copy in scan_c(way, c):
            copy.wait_recv()

    loads[0].wait()
    loads[1].wait()
    doc[...] = jnp.broadcast_to(doc_row[...], doc.shape)
    for c in range(hq):
        hs = chunk_heads(c)
        outs = [dot(lk[:, lanes(h)], lv[:, lanes(h)], 0, 0).astype(bf16) for h in hs]
        for h, o in zip(hs, outs):
            st_own[0, h] = o
        if c == 0:
            pl.semaphore_wait(barrier, (G - 1) + (planes - 1) + (n_tp - 1))
        scan_start(0, c)

    def kv_lanes(r):
        return pl.ds(pl.multiple_of((r * kv_heads // G) * HD, HD), HD)

    def soft_copies(which):
        out = []
        for d in range(1, G):
            r = member(d)
            rows = pl.ds(pl.multiple_of(p * length, length), length)
            refs = (
                (sk.at[:, kv_lanes(r)], kv.at[z, 0, rows]),
                (sv.at[:, kv_lanes(r)], kv.at[z, 1, rows]),
                (doc, doc_in.at[p]),
                (sq.at[:, pl.ds(pl.multiple_of(r * qw, HD), qw)], q_in.at[p]),
            )
            for i in which:
                src, dst = refs[i]
                out.append(
                    remote(src, dst, s_send.at[d - 1, i], s_recv.at[d - 1, i], at_member(r))
                )
        return out

    for load in loads[2:6]:
        load.wait()
    own_rows = pl.ds(pl.multiple_of(p * length, length), length)
    kv[z, 0, own_rows] = sk[:, kv_lanes(p)]
    kv[z, 1, own_rows] = sv[:, kv_lanes(p)]
    doc_in[p] = doc[...]
    q_in[p] = sq[:, pl.ds(pl.multiple_of(p * qw, HD), qw)]

    lower = lax.broadcasted_iota(jnp.int32, (length, length), 0) >= lax.broadcasted_iota(
        jnp.int32, (length, length), 1
    )

    def intra_forward(hs):
        qs = [lq[:, lanes(h)] for h in hs]
        ks = [lk[:, lanes(h)] for h in hs]
        vs = [lv[:, lanes(h)] for h in hs]
        ws = [jnp.where(lower, dot(a, b, 1, 1), 0.0).astype(bf16) for a, b in zip(qs, ks)]
        ms = [dot(w, v, 1, 0) for w, v in zip(ws, vs)]
        for h, w, m in zip(hs, ws, ms):
            scores[h] = w
            mix[:, lanes(h)] = m

    for c in range(hq):
        intra_forward(chunk_heads(c))
        scan_middle(0, c)
        if c == (hq - 1) // 2:
            for copy in soft_copies((0, 1, 2)):
                copy.start()
    for copy in soft_copies((3,)):
        copy.start()
    for copy in soft_copies((0, 1, 2)):
        copy.wait_recv()

    def kv_copy(k):
        return remote(
            kv.at[z], kv.at[z], kvz_send.at[k - 1], kvz_recv.at[k - 1], at_plane(z + k)
        )

    def kv_arrival(k):
        return remote(
            kv.at[z - k], kv.at[z - k], kvz_send.at[k - 1], kvz_recv.at[k - 1], at_plane(z - k)
        )

    for k in range(1, planes):

        @pl.when(z + k < planes)
        def _():
            kv_copy(k).start()

    span = G * length
    factor = math.log2(math.e) / math.sqrt(HD)

    def tile(b, zz, first):
        keys = kv[zz, 0]
        vals = kv[zz, 1]
        raw = dot(keys, q_rows[b], 1, 1) * factor
        key_pos = zz * span + lax.broadcasted_iota(jnp.int32, (span, qw), 0)
        begins = jnp.concatenate([doc_in[b][0:1, :]] * mine, axis=1)
        allowed = key_pos >= begins
        if first:
            one = lax.broadcasted_iota(jnp.int32, (1, length), 1)
            q_pos = z * span + b * length + jnp.concatenate([one] * mine, axis=1)
            allowed = allowed & (key_pos <= q_pos)
        raw = jnp.where(allowed, raw, floor_score)
        high = jnp.max(raw, axis=0, keepdims=True)
        if not first:
            old = top[b]
            high = jnp.maximum(old, high)
            shrink = jnp.exp2(old - high)
        probs = jnp.exp2(raw - high)
        summed = jnp.sum(probs, axis=0, keepdims=True)
        update = dot(vals, probs.astype(bf16), 0, 0)
        top[b] = high
        if first:
            total[b] = summed
            acc[b] = update
        else:
            total[b] = total[b] * shrink + summed
            acc[b] = acc[b] * shrink + update

    def own_tile(b, _):
        for h in range(mine):
            q_rows[b, h * length : (h + 1) * length, :] = q_in[b, :, h * HD : (h + 1) * HD]
        tile(b, z, True)
        return 0

    for c in range(hq):
        scan_end(0, c)
    loads[6].wait()

    ex_own[...] = jnp.zeros_like(ex_own)

    def inter_forward(hs):
        qs = [lq[:, lanes(h)] for h in hs]
        ss = [st_fin[0, h] for h in hs]
        ms = [mix[:, lanes(h)] + dot(a, s, 1, 0) for h, a, s in zip(hs, qs, ss)]
        gs = [lg[:, lanes(h)].astype(f32) for h in hs]
        square, inner = ex_own[0], ex_own[1]
        for m, g in zip(ms, gs):
            square = square + m * m
            inner = inner + g * m
        ex_own[0] = square
        ex_own[1] = inner
        for h, m in zip(hs, ms):
            mix[:, lanes(h)] = m

    for c in range(hq):
        scan_done(0, c)
        inter_forward(chunk_heads(c))

    def exchange():
        return [
            remote(
                ex_own, ex_in.at[k - 1], e_send.at[k - 1], e_recv.at[k - 1],
                {"tp": lax.rem(tp + k, n_tp)},
            )
            for k in range(1, n_tp)
        ]

    for copy in exchange():
        copy.start()
    for copy in exchange():
        copy.wait_recv()
    square, inner = ex_own[0], ex_own[1]
    for k in range(n_tp - 1):
        square = square + ex_in[k, 0]
        inner = inner + ex_in[k, 1]
    features = heads * HD * n_tp
    scale = lax.rsqrt(jnp.sum(square, axis=1, keepdims=True) / features + epsilon)
    mean = scale * jnp.sum(inner, axis=1, keepdims=True) / features

    def turn(hs):
        qs = [lq[:, lanes(h)] for h in hs]
        ns = [mix[:, lanes(h)] * scale for h in hs]
        gs = [(scale * (lg[:, lanes(h)].astype(f32) - m * mean)).astype(bf16) for h, m in zip(hs, ns)]
        adj = [dot(a, g, 0, 0).astype(bf16) for a, g in zip(qs, gs)]
        for h, m, g, o in zip(hs, ns, gs, adj):
            lin_out[:, lanes(h)] = m.astype(bf16)
            gmix[:, lanes(h)] = g
            st_own[1, h] = o

    for c in range(hq):
        turn(chunk_heads(c))
        scan_start(1, c)

    def intra_backward(hs):
        qs = [lq[:, lanes(h)] for h in hs]
        ks = [lk[:, lanes(h)] for h in hs]
        vs = [lv[:, lanes(h)] for h in hs]
        gs = [gmix[:, lanes(h)] for h in hs]
        ss = [st_fin[0, h] for h in hs]
        ws = [scores[h] for h in hs]
        ds = [jnp.where(lower, dot(g, v, 1, 1), 0.0).astype(bf16) for g, v in zip(gs, vs)]
        gq = [dot(d, k, 1, 0) + dot(g, s, 1, 1) for d, k, g, s in zip(ds, ks, gs, ss)]
        gk = [dot(d, q, 0, 0) for d, q in zip(ds, qs)]
        gv = [dot(w, g, 0, 0) for w, g in zip(ws, gs)]
        for h, a, b, c in zip(hs, gq, gk, gv):
            grad_q[:, lanes(h)] = a.astype(bf16)
            gk_acc[:, lanes(h)] = b
            gv_acc[:, lanes(h)] = c

    for c in range(hq):
        intra_backward(chunk_heads(c))
        scan_middle(1, c)

    def earlier_plane(k, _):
        kv_arrival(k).wait_recv()

        def one(b, _):
            tile(b, z - k, False)
            return 0

        lax.fori_loop(0, G, one, 0)
        return 0

    def finish(b, _):
        out = acc[b] / total[b]
        for h in range(mine):
            o_own[b, :, h * HD : (h + 1) * HD] = jnp.transpose(
                out[:, h * length : (h + 1) * length]
            ).astype(bf16)
        return 0

    def out_copies():
        return [
            remote(
                o_own.at[member(d)], soft_out.at[:, pl.ds(pl.multiple_of(p * qw, HD), qw)],
                o_send.at[d - 1], o_recv.at[d - 1], at_member(member(d)),
            )
            for d in range(1, G)
        ]

    for copy in soft_copies((3,)):
        copy.wait_recv()

    def soft_rest():
        lax.fori_loop(0, G, own_tile, 0)
        lax.fori_loop(1, z + 1, earlier_plane, 0)
        lax.fori_loop(0, G, finish, 0)
        for copy in out_copies():
            copy.start()
        soft_out[:, pl.ds(pl.multiple_of(p * qw, HD), qw)] = o_own[p]

    pl.when(z < planes // 2)(soft_rest)
    for c in range(hq):
        scan_end(1, c)
    pl.when(z >= planes // 2)(soft_rest)

    def inter_backward(hs):
        ks = [lk[:, lanes(h)] for h in hs]
        vs = [lv[:, lanes(h)] for h in hs]
        ss = [st_fin[1, h] for h in hs]
        gk = [gk_acc[:, lanes(h)] + dot(v, s, 1, 1) for h, v, s in zip(hs, vs, ss)]
        gv = [gv_acc[:, lanes(h)] + dot(k, s, 1, 0) for h, k, s in zip(hs, ks, ss)]
        for h, a, b in zip(hs, gk, gv):
            grad_k[:, lanes(h)] = a.astype(bf16)
            grad_v[:, lanes(h)] = b.astype(bf16)

    for c in range(hq):
        scan_done(1, c)
        inter_backward(chunk_heads(c))

    for copy in out_copies():
        copy.wait_recv()
    for way in (0, 1):
        for c in range(hq):
            for copy in scan_a(way, c) + scan_c(way, c):
                copy.wait_send()
    for copy in soft_copies((0, 1, 2, 3)) + exchange() + out_copies():
        copy.wait_send()
    for k in range(1, planes):

        @pl.when(z + k < planes)
        def _():
            kv_copy(k).wait_send()

        for way in (0, 1):

            @pl.when(sends_z(way, k))
            def _():
                for c in range(hq):
                    scan_z(way, k, c).wait_send()


def on_device(n, n_tp, lq, lk, lv, lg, sq, sk, sv, doc_start):
    length, width = lq.shape
    heads = width // HD
    hq = heads // G
    planes = n // G
    q_width = sq.shape[1]
    qw = q_width // G
    doc_row = doc_start.reshape(1, length)
    dma = pltpu.SemaphoreType.DMA
    vm = pltpu.VMEM
    span = G * length
    others = planes - 1
    kv_width = sk.shape[1]
    scratch = [
        vm((length, width), bf16), vm((length, width), bf16),
        vm((length, width), bf16), vm((length, width), bf16),
        vm((length, q_width), bf16), vm((length, kv_width), bf16), vm((length, kv_width), bf16),
        vm((8, length), jnp.int32),
        dma((7,)),
        vm((2, heads, HD, HD), bf16),
        vm((2, G, hq, HD, HD), bf16),
        vm((2, hq, HD, HD), bf16),
        vm((2, others, hq, HD, HD), bf16),
        vm((2, G, hq, HD, HD), bf16),
        vm((2, heads, HD, HD), bf16),
        vm((heads, length, length), bf16),
        vm((length, width), f32),
        vm((length, width), bf16),
        vm((length, width), f32),
        vm((length, width), f32),
        vm((2, length, HD), f32),
        vm((n_tp - 1, 2, length, HD), f32),
        vm((planes, 2, span, HD), bf16),
        vm((G, length, qw), bf16),
        vm((G, qw // HD * length, HD), bf16),
        vm((G, 8, length), jnp.int32),
        vm((G, length, qw), bf16),
        vm((G, 1, qw), f32),
        vm((G, 1, qw), f32),
        vm((G, HD, qw), f32),
        vm((HD, HD), f32),
        dma((2, G - 1, hq)), dma((2, G - 1, hq)),
        dma((2, others, hq)), dma((2, others, hq)),
        dma((2, G - 1, hq)), dma((2, G - 1, hq)),
        dma((n_tp - 1,)), dma((n_tp - 1,)),
        dma((G - 1, 4)), dma((G - 1, 4)),
        dma((others,)), dma((others,)),
        dma((G - 1,)), dma((G - 1,)),
    ]
    hbm = pl.BlockSpec(memory_space=pl.ANY)
    here = pl.BlockSpec(memory_space=pltpu.VMEM)
    widths = [width] * 4 + [q_width]
    held = pl.pallas_call(
        functools.partial(kernel, n, n_tp),
        out_shape=[pltpu.VMEM((length, w), bf16) for w in widths],
        in_specs=[hbm] * 7 + [here],
        out_specs=[here] * 5,
        scratch_shapes=scratch,
        compiler_params=pltpu.CompilerParams(
            collective_id=0, has_side_effects=True, vmem_limit_bytes=52 * 1024 * 1024
        ),
    )(lq, lk, lv, lg, sq, sk, sv, doc_row)
    return pl.pallas_call(
        write_out,
        out_shape=[jax.ShapeDtypeStruct((length, w), bf16) for w in widths],
        in_specs=[here] * 5,
        out_specs=[hbm] * 5,
        scratch_shapes=[dma((5,))],
    )(*held)


def write_out(*refs):
    sems = refs[10]
    copies = [pltpu.make_async_copy(refs[i], refs[5 + i], sems.at[i]) for i in range(5)]
    for copy in copies:
        copy.start()
    for copy in copies:
        copy.wait()


def solution(mesh):
    wide = P("ctx", "tp")
    return jax.shard_map(
        functools.partial(on_device, mesh.shape["ctx"], mesh.shape["tp"]),
        mesh=mesh,
        in_specs=(wide,) * 7 + (P("ctx"),),
        out_specs=(wide,) * 5,
        check_vma=False,
    )
```

```python
import functools
import math

import jax
import jax.numpy as jnp
from jax import lax
from jax.experimental import pallas as pl
from jax.experimental.pallas import tpu as pltpu
from jax.sharding import PartitionSpec as P

HD = 128
G = 4

MESH = pl.DeviceIdType.MESH
epsilon = 1e-06
floor_score = -1e30
f32 = jnp.float32
bf16 = jnp.bfloat16


def dot(a, b, ca, cb):
    return lax.dot_general(a, b, (((ca,), (cb,)), ((), ())), preferred_element_type=f32)


def kernel(
    n,
    n_tp,
    lq_hbm, lk_hbm, lv_hbm, lg_hbm, sq_hbm, sk_hbm, sv_hbm, doc_row,
    lin_out, grad_q, grad_k, grad_v, soft_out,
    lq, lk, lv, lg, sq, sk, sv, doc, in_sems,
    st_own, st_in, st_tot, st_z, st_out, st_fin,
    scores, mix, gmix, gk_acc, gv_acc,
    ex_own, ex_in,
    kv, q_in, q_rows, doc_in, o_own, top, total, acc, carry_ref,
    a_send, a_recv, z_send, z_recv, c_send, c_recv,
    e_send, e_recv, s_send, s_recv, kvz_send, kvz_recv, o_send, o_recv,
):
    loads = [
        pltpu.make_async_copy(src, dst, in_sems.at[i])
        for i, (src, dst) in enumerate(
            (
                (lk_hbm, lk), (lv_hbm, lv), (lq_hbm, lq), (sk_hbm, sk),
                (sv_hbm, sv), (sq_hbm, sq), (lg_hbm, lg),
            )
        )
    ]
    for copy in loads:
        copy.start()
    length = lq.shape[0]
    heads = lq.shape[1] // HD
    hq = heads // G
    planes = n // G
    q_heads = sq.shape[1] // HD
    kv_heads = sk.shape[1] // HD
    mine = q_heads // G
    qw = mine * HD
    me = lax.axis_index("ctx")
    tp = lax.axis_index("tp")
    z = me // G
    p = lax.rem(me, G)

    def member(d):
        return lax.rem(p + d, G)

    def at_member(r):
        return {"ctx": z * G + r}

    def at_plane(zz):
        return {"ctx": zz * G + p}

    def remote(src, dst, send, recv, device):
        return pltpu.make_async_remote_copy(
            src_ref=src, dst_ref=dst, send_sem=send, recv_sem=recv,
            device_id=device, device_id_type=MESH,
        )

    barrier = pltpu.get_barrier_semaphore()
    for d in range(1, G):
        pl.semaphore_signal(barrier, inc=1, device_id=at_member(member(d)), device_id_type=MESH)
    for k in range(1, planes):
        pl.semaphore_signal(
            barrier, inc=1, device_id=at_plane(lax.rem(z + k, planes)), device_id_type=MESH
        )
    for k in range(1, n_tp):
        pl.semaphore_signal(
            barrier, inc=1, device_id={"tp": lax.rem(tp + k, n_tp)}, device_id_type=MESH
        )

    def lanes(h):
        return pl.ds(pl.multiple_of(h * HD, HD), HD)

    def chunk_heads(c):
        return [r * hq + c for r in range(G)]

    def per_chunk(body):
        for c in range(hq):
            body(chunk_heads(c))

    def per_chunk_loop(body):
        def step(c, _):
            body(chunk_heads(c))
            return 0

        lax.fori_loop(0, hq, step, 0)

    def scan_a(way, c):
        return [
            remote(
                st_own.at[way, member(d) * hq + c], st_in.at[way, p, c],
                a_send.at[way, d - 1, c], a_recv.at[way, d - 1, c], at_member(member(d)),
            )
            for d in range(1, G)
        ]

    def scan_z(way, k, c):
        there = z - k if way else z + k
        return remote(
            st_tot.at[way, c], st_z.at[way, k - 1, c],
            z_send.at[way, k - 1, c], z_recv.at[way, k - 1, c], at_plane(there),
        )

    def sends_z(way, k):
        return (z - k >= 0) if way else (z + k < planes)

    def scan_c(way, c):
        return [
            remote(
                st_out.at[way, member(d), c], st_fin.at[way, p * hq + c],
                c_send.at[way, d - 1, c], c_recv.at[way, d - 1, c], at_member(member(d)),
            )
            for d in range(1, G)
        ]

    def scan_start(way, c):
        for copy in scan_a(way, c):
            copy.start()
        st_in[way, p, c] = st_own[way, p * hq + c]

    def scan_middle(way, c):
        for copy in scan_a(way, c):
            copy.wait_recv()
        parts = [st_in[way, s, c].astype(f32) for s in range(G)]
        st_tot[way, c] = ((parts[0] + parts[1]) + (parts[2] + parts[3])).astype(bf16)
        for k in range(1, planes):

            @pl.when(sends_z(way, k))
            def _():
                scan_z(way, k, c).start()

    def scan_end(way, c):
        carry_ref[...] = jnp.zeros((HD, HD), f32)
        for k in range(1, planes):

            @pl.when(sends_z(1 - way, k))
            def _():
                scan_z(way, k, c).wait_recv()
                carry_ref[...] += st_z[way, k - 1, c].astype(f32)

        carry = carry_ref[...]
        order = range(G - 1, -1, -1) if way else range(G)
        for s in order:
            st_out[way, s, c] = carry.astype(bf16)
            carry = carry + st_in[way, s, c].astype(f32)
        for copy in scan_c(way, c):
            copy.start()
        st_fin[way, p * hq + c] = st_out[way, p, c]

    def scan_done(way, c):
        for copy in scan_c(way, c):
            copy.wait_recv()

    loads[0].wait()
    loads[1].wait()
    doc[...] = jnp.broadcast_to(doc_row[...], doc.shape)
    for c in range(hq):
        hs = chunk_heads(c)
        outs = [dot(lk[:, lanes(h)], lv[:, lanes(h)], 0, 0).astype(bf16) for h in hs]
        for h, o in zip(hs, outs):
            st_own[0, h] = o
        if c == 0:
            pl.semaphore_wait(barrier, (G - 1) + (planes - 1) + (n_tp - 1))
        scan_start(0, c)

    def kv_lanes(r):
        return pl.ds(pl.multiple_of((r * kv_heads // G) * HD, HD), HD)

    def soft_copies(which):
        out = []
        for d in range(1, G):
            r = member(d)
            rows = pl.ds(pl.multiple_of(p * length, length), length)
            refs = (
                (sk.at[:, kv_lanes(r)], kv.at[z, 0, rows]),
                (sv.at[:, kv_lanes(r)], kv.at[z, 1, rows]),
                (doc, doc_in.at[p]),
                (sq.at[:, pl.ds(pl.multiple_of(r * qw, HD), qw)], q_in.at[p]),
            )
            for i in which:
                src, dst = refs[i]
                out.append(
                    remote(src, dst, s_send.at[d - 1, i], s_recv.at[d - 1, i], at_member(r))
                )
        return out

    for load in loads[2:6]:
        load.wait()
    own_rows = pl.ds(pl.multiple_of(p * length, length), length)
    kv[z, 0, own_rows] = sk[:, kv_lanes(p)]
    kv[z, 1, own_rows] = sv[:, kv_lanes(p)]
    doc_in[p] = doc[...]
    q_in[p] = sq[:, pl.ds(pl.multiple_of(p * qw, HD), qw)]

    lower = lax.broadcasted_iota(jnp.int32, (length, length), 0) >= lax.broadcasted_iota(
        jnp.int32, (length, length), 1
    )

    def intra_forward(hs):
        qs = [lq[:, lanes(h)] for h in hs]
        ks = [lk[:, lanes(h)] for h in hs]
        vs = [lv[:, lanes(h)] for h in hs]
        ws = [jnp.where(lower, dot(a, b, 1, 1), 0.0).astype(bf16) for a, b in zip(qs, ks)]
        ms = [dot(w, v, 1, 0) for w, v in zip(ws, vs)]
        for h, w, m in zip(hs, ws, ms):
            scores[h] = w
            mix[:, lanes(h)] = m

    for c in range(hq):
        intra_forward(chunk_heads(c))
        scan_middle(0, c)
        if c == (hq - 1) // 2:
            for copy in soft_copies((0, 1, 2)):
                copy.start()
    for copy in soft_copies((0, 1, 2)):
        copy.wait_recv()

    def kv_copy(k):
        return remote(
            kv.at[z], kv.at[z], kvz_send.at[k - 1], kvz_recv.at[k - 1], at_plane(z + k)
        )

    def kv_arrival(k):
        return remote(
            kv.at[z - k], kv.at[z - k], kvz_send.at[k - 1], kvz_recv.at[k - 1], at_plane(z - k)
        )

    for k in range(1, planes):

        @pl.when(z + k < planes)
        def _():
            kv_copy(k).start()

    span = G * length
    factor = math.log2(math.e) / math.sqrt(HD)

    def tile(b, zz, first, count):
        keys = kv[zz, 0, :count]
        vals = kv[zz, 1, :count]
        raw = dot(keys, q_rows[...], 1, 1) * factor
        row = lax.broadcasted_iota(jnp.int32, (count, qw), 0)
        begins = jnp.concatenate([doc_in[b][0:1, :]] * mine, axis=1)
        allowed = row >= begins - zz * span
        if first:
            one = lax.broadcasted_iota(jnp.int32, (1, length), 1)
            allowed = allowed & (row <= b * length + jnp.concatenate([one] * mine, axis=1))
        raw = jnp.where(allowed, raw, floor_score)
        high = jnp.max(raw, axis=0, keepdims=True)
        if not first:
            old = top[...]
            high = jnp.maximum(old, high)
            shrink = jnp.exp2(old - high)
        probs = jnp.exp2(raw - high)
        summed = jnp.sum(probs, axis=0, keepdims=True)
        update = dot(vals, probs.astype(bf16), 0, 0)
        top[...] = high
        if first:
            total[...] = summed
            acc[...] = update
        else:
            total[...] = total[...] * shrink + summed
            acc[...] = acc[...] * shrink + update

    def out_copy(b, d):
        return remote(
            o_own.at[b], soft_out.at[:, pl.ds(pl.multiple_of(p * qw, HD), qw)],
            o_send.at[d], o_recv.at[d], at_member(b),
        )

    def query_block(i, _):
        b = member(i + 1)
        for h in range(mine):
            q_rows[h * length : (h + 1) * length, :] = q_in[b, :, h * HD : (h + 1) * HD]

        @pl.when(b < G // 2)
        def _():
            tile(b, z, True, span // 2)

        @pl.when(b >= G // 2)
        def _():
            tile(b, z, True, span)

        def earlier_plane(k, _):
            @pl.when(i == 0)
            def _():
                kv_arrival(k).wait_recv()

            tile(b, z - k, False, span)
            return 0

        lax.fori_loop(1, z + 1, earlier_plane, 0)
        out = acc[...] / total[...]
        for h in range(mine):
            o_own[b, :, h * HD : (h + 1) * HD] = jnp.transpose(
                out[:, h * length : (h + 1) * length]
            ).astype(bf16)

        @pl.when(i < G - 1)
        def _():
            out_copy(b, i).start()

        return 0

    for c in range(hq):
        scan_end(0, c)
    for copy in soft_copies((3,)):
        copy.start()
    loads[6].wait()

    ex_own[...] = jnp.zeros_like(ex_own)

    def inter_forward(hs):
        qs = [lq[:, lanes(h)] for h in hs]
        ss = [st_fin[0, h] for h in hs]
        ms = [mix[:, lanes(h)] + dot(a, s, 1, 0) for h, a, s in zip(hs, qs, ss)]
        gs = [lg[:, lanes(h)].astype(f32) for h in hs]
        square, inner = ex_own[0], ex_own[1]
        for m, g in zip(ms, gs):
            square = square + m * m
            inner = inner + g * m
        ex_own[0] = square
        ex_own[1] = inner
        for h, m in zip(hs, ms):
            mix[:, lanes(h)] = m

    for c in range(hq):
        scan_done(0, c)
        inter_forward(chunk_heads(c))

    def exchange():
        return [
            remote(
                ex_own, ex_in.at[k - 1], e_send.at[k - 1], e_recv.at[k - 1],
                {"tp": lax.rem(tp + k, n_tp)},
            )
            for k in range(1, n_tp)
        ]

    for copy in exchange():
        copy.start()
    for copy in exchange():
        copy.wait_recv()
    square, inner = ex_own[0], ex_own[1]
    for k in range(n_tp - 1):
        square = square + ex_in[k, 0]
        inner = inner + ex_in[k, 1]
    features = heads * HD * n_tp
    scale = lax.rsqrt(jnp.sum(square, axis=1, keepdims=True) / features + epsilon)
    mean = scale * jnp.sum(inner, axis=1, keepdims=True) / features

    def turn(hs):
        qs = [lq[:, lanes(h)] for h in hs]
        ns = [mix[:, lanes(h)] * scale for h in hs]
        gs = [(scale * (lg[:, lanes(h)].astype(f32) - m * mean)).astype(bf16) for h, m in zip(hs, ns)]
        adj = [dot(a, g, 0, 0).astype(bf16) for a, g in zip(qs, gs)]
        for h, m, g, o in zip(hs, ns, gs, adj):
            lin_out[:, lanes(h)] = m.astype(bf16)
            gmix[:, lanes(h)] = g
            st_own[1, h] = o

    for c in range(hq):
        turn(chunk_heads(c))
        scan_start(1, c)

    def intra_backward(hs):
        qs = [lq[:, lanes(h)] for h in hs]
        ks = [lk[:, lanes(h)] for h in hs]
        vs = [lv[:, lanes(h)] for h in hs]
        gs = [gmix[:, lanes(h)] for h in hs]
        ss = [st_fin[0, h] for h in hs]
        ws = [scores[h] for h in hs]
        ds = [jnp.where(lower, dot(g, v, 1, 1), 0.0).astype(bf16) for g, v in zip(gs, vs)]
        gq = [dot(d, k, 1, 0) + dot(g, s, 1, 1) for d, k, g, s in zip(ds, ks, gs, ss)]
        gk = [dot(d, q, 0, 0) for d, q in zip(ds, qs)]
        gv = [dot(w, g, 0, 0) for w, g in zip(ws, gs)]
        for h, a, b, c in zip(hs, gq, gk, gv):
            grad_q[:, lanes(h)] = a.astype(bf16)
            gk_acc[:, lanes(h)] = b
            gv_acc[:, lanes(h)] = c

    for c in range(hq):
        intra_backward(chunk_heads(c))
        scan_middle(1, c)

    for copy in soft_copies((3,)):
        copy.wait_recv()
    ahead = jnp.where(z < planes // 2, G, jnp.where(z < planes - 1, 1, 0))
    lax.fori_loop(0, ahead, query_block, 0)
    for c in range(hq):
        scan_end(1, c)
    lax.fori_loop(ahead, G, query_block, 0)
    soft_out[:, pl.ds(pl.multiple_of(p * qw, HD), qw)] = o_own[p]

    def inter_backward(hs):
        ks = [lk[:, lanes(h)] for h in hs]
        vs = [lv[:, lanes(h)] for h in hs]
        ss = [st_fin[1, h] for h in hs]
        gk = [gk_acc[:, lanes(h)] + dot(v, s, 1, 1) for h, v, s in zip(hs, vs, ss)]
        gv = [gv_acc[:, lanes(h)] + dot(k, s, 1, 0) for h, k, s in zip(hs, ks, ss)]
        for h, a, b in zip(hs, gk, gv):
            grad_k[:, lanes(h)] = a.astype(bf16)
            grad_v[:, lanes(h)] = b.astype(bf16)

    for c in range(hq):
        scan_done(1, c)
        inter_backward(chunk_heads(c))

    out_copies = [out_copy(member(d + 1), d) for d in range(G - 1)]
    for copy in out_copies:
        copy.wait_recv()
    for way in (0, 1):
        for c in range(hq):
            for copy in scan_a(way, c) + scan_c(way, c):
                copy.wait_send()
    for copy in soft_copies((0, 1, 2, 3)) + exchange() + out_copies:
        copy.wait_send()
    for k in range(1, planes):

        @pl.when(z + k < planes)
        def _():
            kv_copy(k).wait_send()

        for way in (0, 1):

            @pl.when(sends_z(way, k))
            def _():
                for c in range(hq):
                    scan_z(way, k, c).wait_send()


def on_device(n, n_tp, lq, lk, lv, lg, sq, sk, sv, doc_start):
    length, width = lq.shape
    heads = width // HD
    hq = heads // G
    planes = n // G
    q_width = sq.shape[1]
    qw = q_width // G
    doc_row = doc_start.reshape(1, length)
    dma = pltpu.SemaphoreType.DMA
    vm = pltpu.VMEM
    span = G * length
    others = planes - 1
    kv_width = sk.shape[1]
    scratch = [
        vm((length, width), bf16), vm((length, width), bf16),
        vm((length, width), bf16), vm((length, width), bf16),
        vm((length, q_width), bf16), vm((length, kv_width), bf16), vm((length, kv_width), bf16),
        vm((8, length), jnp.int32),
        dma((7,)),
        vm((2, heads, HD, HD), bf16),
        vm((2, G, hq, HD, HD), bf16),
        vm((2, hq, HD, HD), bf16),
        vm((2, others, hq, HD, HD), bf16),
        vm((2, G, hq, HD, HD), bf16),
        vm((2, heads, HD, HD), bf16),
        vm((heads, length, length), bf16),
        vm((length, width), f32),
        vm((length, width), bf16),
        vm((length, width), f32),
        vm((length, width), f32),
        vm((2, length, HD), f32),
        vm((n_tp - 1, 2, length, HD), f32),
        vm((planes, 2, span, HD), bf16),
        vm((G, length, qw), bf16),
        vm((qw // HD * length, HD), bf16),
        vm((G, 8, length), jnp.int32),
        vm((G, length, qw), bf16),
        vm((1, qw), f32),
        vm((1, qw), f32),
        vm((HD, qw), f32),
        vm((HD, HD), f32),
        dma((2, G - 1, hq)), dma((2, G - 1, hq)),
        dma((2, others, hq)), dma((2, others, hq)),
        dma((2, G - 1, hq)), dma((2, G - 1, hq)),
        dma((n_tp - 1,)), dma((n_tp - 1,)),
        dma((G - 1, 4)), dma((G - 1, 4)),
        dma((others,)), dma((others,)),
        dma((G - 1,)), dma((G - 1,)),
    ]
    hbm = pl.BlockSpec(memory_space=pl.ANY)
    here = pl.BlockSpec(memory_space=pltpu.VMEM)
    widths = [width] * 4 + [q_width]
    held = pl.pallas_call(
        functools.partial(kernel, n, n_tp),
        out_shape=[pltpu.VMEM((length, w), bf16) for w in widths],
        in_specs=[hbm] * 7 + [here],
        out_specs=[here] * 5,
        scratch_shapes=scratch,
        compiler_params=pltpu.CompilerParams(
            collective_id=0, has_side_effects=True, vmem_limit_bytes=52 * 1024 * 1024
        ),
    )(lq, lk, lv, lg, sq, sk, sv, doc_row)
    return pl.pallas_call(
        write_out,
        out_shape=[jax.ShapeDtypeStruct((length, w), bf16) for w in widths],
        in_specs=[here] * 5,
        out_specs=[hbm] * 5,
        scratch_shapes=[dma((5,))],
        compiler_params=pltpu.CompilerParams(vmem_limit_bytes=8 * 1024 * 1024),
    )(*held)


def write_out(*refs):
    sems = refs[10]
    copies = [pltpu.make_async_copy(refs[i], refs[5 + i], sems.at[i]) for i in range(5)]
    for copy in copies:
        copy.start()
    for copy in copies:
        copy.wait()


def solution(mesh):
    wide = P("ctx", "tp")
    return jax.shard_map(
        functools.partial(on_device, mesh.shape["ctx"], mesh.shape["tp"]),
        mesh=mesh,
        in_specs=(wide,) * 7 + (P("ctx"),),
        out_specs=(wide,) * 5,
        check_vma=False,
    )
```

```python
import functools
import math

import jax
import jax.numpy as jnp
from jax import lax
from jax.experimental import pallas as pl
from jax.experimental.pallas import tpu as pltpu
from jax.sharding import PartitionSpec as P

HD = 128
G = 4

MESH = pl.DeviceIdType.MESH
epsilon = 1e-06
floor_score = -1e30
f32 = jnp.float32
bf16 = jnp.bfloat16


def dot(a, b, ca, cb):
    return lax.dot_general(a, b, (((ca,), (cb,)), ((), ())), preferred_element_type=f32)


def kernel(
    n,
    n_tp,
    lq_hbm, lk_hbm, lv_hbm, lg_hbm, sq_hbm, sk_hbm, sv_hbm, doc_row,
    lin_out, grad_q, grad_k, grad_v, soft_out,
    lq, lk, lv, lg, sq, sk, sv, doc, in_sems,
    st_own, st_in, st_tot, st_z, st_out, st_fin,
    scores, mix, gmix, gk_acc, gv_acc,
    ex_own, ex_in,
    kv, q_in, q_rows, doc_in, o_own, top, total, acc, carry_ref, st_sum,
    a_send, a_recv, z_send, z_recv, c_send, c_recv,
    e_send, e_recv, s_send, s_recv, kvz_send, kvz_recv, o_send, o_recv,
):
    loads = [
        pltpu.make_async_copy(src, dst, in_sems.at[i])
        for i, (src, dst) in enumerate(
            (
                (lk_hbm, lk), (lv_hbm, lv), (lq_hbm, lq), (sk_hbm, sk),
                (sv_hbm, sv), (sq_hbm, sq), (lg_hbm, lg),
            )
        )
    ]
    for copy in loads:
        copy.start()
    length = lq.shape[0]
    heads = lq.shape[1] // HD
    hq = heads // G
    planes = n // G
    q_heads = sq.shape[1] // HD
    kv_heads = sk.shape[1] // HD
    mine = q_heads // G
    qw = mine * HD
    me = lax.axis_index("ctx")
    tp = lax.axis_index("tp")
    z = me // G
    p = lax.rem(me, G)

    def member(d):
        return lax.rem(p + d, G)

    def at_member(r):
        return {"ctx": z * G + r}

    def at_plane(zz):
        return {"ctx": zz * G + p}

    def remote(src, dst, send, recv, device):
        return pltpu.make_async_remote_copy(
            src_ref=src, dst_ref=dst, send_sem=send, recv_sem=recv,
            device_id=device, device_id_type=MESH,
        )

    barrier = pltpu.get_barrier_semaphore()
    for d in range(1, G):
        pl.semaphore_signal(barrier, inc=1, device_id=at_member(member(d)), device_id_type=MESH)
    for step, there in ((1, z + 1 < planes), (-1, z > 0)):

        @pl.when(there)
        def _():
            pl.semaphore_signal(
                barrier, inc=1, device_id=at_plane(z + step), device_id_type=MESH
            )

    for k in range(1, n_tp):
        pl.semaphore_signal(
            barrier, inc=1, device_id={"tp": lax.rem(tp + k, n_tp)}, device_id_type=MESH
        )

    def lanes(h):
        return pl.ds(pl.multiple_of(h * HD, HD), HD)

    def chunk_heads(c):
        return [r * hq + c for r in range(G)]

    def per_chunk(body):
        for c in range(hq):
            body(chunk_heads(c))

    def per_chunk_loop(body):
        def step(c, _):
            body(chunk_heads(c))
            return 0

        lax.fori_loop(0, hq, step, 0)

    def scan_a(way, c):
        return [
            remote(
                st_own.at[way, member(d) * hq + c], st_in.at[way, p, c],
                a_send.at[way, d - 1, c], a_recv.at[way, d - 1, c], at_member(member(d)),
            )
            for d in range(1, G)
        ]

    def scan_z(way, c):
        return remote(
            st_tot.at[way, c], st_z.at[way, c], z_send.at[way, c], z_recv.at[way, c],
            at_plane(z - 1 if way else z + 1),
        )

    def passes_on(way):
        return z > 0 if way else z + 1 < planes

    def is_passed(way):
        return passes_on(1 - way)

    def scan_c(way, c):
        return [
            remote(
                st_out.at[way, member(d), c], st_fin.at[way, p * hq + c],
                c_send.at[way, d - 1, c], c_recv.at[way, d - 1, c], at_member(member(d)),
            )
            for d in range(1, G)
        ]

    def scan_start(way, c):
        for copy in scan_a(way, c):
            copy.start()
        st_in[way, p, c] = st_own[way, p * hq + c]

    def scan_middle(way, c):
        for copy in scan_a(way, c):
            copy.wait_recv()
        parts = [st_in[way, s, c].astype(f32) for s in range(G)]
        st_sum[c] = (parts[0] + parts[1]) + (parts[2] + parts[3])

        @pl.when(passes_on(way) & jnp.logical_not(is_passed(way)))
        def _():
            st_tot[way, c] = st_sum[c].astype(bf16)
            scan_z(way, c).start()

    def scan_end(way, c):
        carry_ref[...] = jnp.zeros((HD, HD), f32)

        @pl.when(is_passed(way))
        def _():
            scan_z(way, c).wait_recv()
            carry_ref[...] = st_z[way, c].astype(f32)

        @pl.when(is_passed(way) & passes_on(way))
        def _():
            st_tot[way, c] = (carry_ref[...] + st_sum[c]).astype(bf16)
            scan_z(way, c).start()

        carry = carry_ref[...]
        order = range(G - 1, -1, -1) if way else range(G)
        for s in order:
            st_out[way, s, c] = carry.astype(bf16)
            carry = carry + st_in[way, s, c].astype(f32)
        for copy in scan_c(way, c):
            copy.start()
        st_fin[way, p * hq + c] = st_out[way, p, c]

    def scan_done(way, c):
        for copy in scan_c(way, c):
            copy.wait_recv()

    loads[0].wait()
    loads[1].wait()
    doc[...] = jnp.broadcast_to(doc_row[...], doc.shape)
    for c in range(hq):
        hs = chunk_heads(c)
        outs = [dot(lk[:, lanes(h)], lv[:, lanes(h)], 0, 0).astype(bf16) for h in hs]
        for h, o in zip(hs, outs):
            st_own[0, h] = o
        if c == 0:
            near = jnp.where(z + 1 < planes, 1, 0) + jnp.where(z > 0, 1, 0)
            pl.semaphore_wait(barrier, (G - 1) + (n_tp - 1) + near)
        scan_start(0, c)

    def kv_lanes(r):
        return pl.ds(pl.multiple_of((r * kv_heads // G) * HD, HD), HD)

    def soft_copies(which):
        out = []
        for d in range(1, G):
            r = member(d)
            rows = pl.ds(pl.multiple_of(p * length, length), length)
            refs = (
                (sk.at[:, kv_lanes(r)], kv.at[z, 0, rows]),
                (sv.at[:, kv_lanes(r)], kv.at[z, 1, rows]),
                (doc, doc_in.at[p]),
                (sq.at[:, pl.ds(pl.multiple_of(r * qw, HD), qw)], q_in.at[p]),
            )
            for i in which:
                src, dst = refs[i]
                out.append(
                    remote(src, dst, s_send.at[d - 1, i], s_recv.at[d - 1, i], at_member(r))
                )
        return out

    for load in loads[2:6]:
        load.wait()
    own_rows = pl.ds(pl.multiple_of(p * length, length), length)
    kv[z, 0, own_rows] = sk[:, kv_lanes(p)]
    kv[z, 1, own_rows] = sv[:, kv_lanes(p)]
    doc_in[p] = doc[...]
    q_in[p] = sq[:, pl.ds(pl.multiple_of(p * qw, HD), qw)]

    lower = lax.broadcasted_iota(jnp.int32, (length, length), 0) >= lax.broadcasted_iota(
        jnp.int32, (length, length), 1
    )

    def intra_forward(hs):
        qs = [lq[:, lanes(h)] for h in hs]
        ks = [lk[:, lanes(h)] for h in hs]
        vs = [lv[:, lanes(h)] for h in hs]
        ws = [jnp.where(lower, dot(a, b, 1, 1), 0.0).astype(bf16) for a, b in zip(qs, ks)]
        ms = [dot(w, v, 1, 0) for w, v in zip(ws, vs)]
        for h, w, m in zip(hs, ws, ms):
            scores[h] = w
            mix[:, lanes(h)] = m

    last = z == planes - 1

    def soft_start(which):
        for copy in soft_copies(which):
            copy.start()

    pl.when(last)(lambda: soft_start((3,)))
    pl.when(jnp.logical_not(last))(lambda: soft_start((0, 1, 2)))
    for c in range(hq):
        intra_forward(chunk_heads(c))

    def kv_hop(k):
        block = kv.at[z - k + 1]
        return remote(block, block, kvz_send.at[k - 1], kvz_recv.at[k - 1], at_plane(z + 1))

    def kv_arrival(k):
        block = kv.at[z - k]
        return remote(block, block, kvz_send.at[k - 1], kvz_recv.at[k - 1], at_plane(z - 1))

    def hops(k):
        return (z + 1 < planes) & (z - k + 1 >= 0)

    def kv_pass(k):
        @pl.when(hops(k))
        def _():
            if k == 1:
                for copy in soft_copies((0, 1, 2)):
                    copy.wait_recv()
            else:
                kv_arrival(k - 1).wait_recv()
            kv_hop(k).start()

    span = G * length
    factor = math.log2(math.e) / math.sqrt(HD)

    def tile(b, zz, first, count):
        keys = kv[zz, 0, :count]
        vals = kv[zz, 1, :count]
        raw = dot(keys, q_rows[...], 1, 1) * factor
        row = lax.broadcasted_iota(jnp.int32, (count, qw), 0)
        begins = jnp.concatenate([doc_in[b][0:1, :]] * mine, axis=1)
        allowed = row >= begins - zz * span
        if first:
            one = lax.broadcasted_iota(jnp.int32, (1, length), 1)
            allowed = allowed & (row <= b * length + jnp.concatenate([one] * mine, axis=1))
        raw = jnp.where(allowed, raw, floor_score)
        high = jnp.max(raw, axis=0, keepdims=True)
        if not first:
            old = top[...]
            high = jnp.maximum(old, high)
            shrink = jnp.exp2(old - high)
        probs = jnp.exp2(raw - high)
        summed = jnp.sum(probs, axis=0, keepdims=True)
        update = dot(vals, probs.astype(bf16), 0, 0)
        top[...] = high
        if first:
            total[...] = summed
            acc[...] = update
        else:
            total[...] = total[...] * shrink + summed
            acc[...] = acc[...] * shrink + update

    def out_copy(b, d):
        return remote(
            o_own.at[b], soft_out.at[:, pl.ds(pl.multiple_of(p * qw, HD), qw)],
            o_send.at[d], o_recv.at[d], at_member(b),
        )

    def query_block(i, _):
        b = member(i + 1)
        for h in range(mine):
            q_rows[h * length : (h + 1) * length, :] = q_in[b, :, h * HD : (h + 1) * HD]

        @pl.when(b < G // 2)
        def _():
            tile(b, z, True, span // 2)

        @pl.when(b >= G // 2)
        def _():
            tile(b, z, True, span)

        def earlier_plane(k, _):
            @pl.when((i == 0) & jnp.logical_not(hops(k + 1)))
            def _():
                kv_arrival(k).wait_recv()

            tile(b, z - k, False, span)
            return 0

        lax.fori_loop(1, z + 1, earlier_plane, 0)
        out = acc[...] / total[...]
        for h in range(mine):
            o_own[b, :, h * HD : (h + 1) * HD] = jnp.transpose(
                out[:, h * length : (h + 1) * length]
            ).astype(bf16)

        @pl.when(i < G - 1)
        def _():
            out_copy(b, i).start()

        return 0

    for c in range(hq):
        scan_middle(0, c)
        scan_end(0, c)
    pl.when(last)(lambda: soft_start((0, 1, 2)))
    pl.when(jnp.logical_not(last))(lambda: soft_start((3,)))
    kv_pass(1)
    loads[6].wait()

    ex_own[...] = jnp.zeros_like(ex_own)

    def inter_forward(hs):
        qs = [lq[:, lanes(h)] for h in hs]
        ss = [st_fin[0, h] for h in hs]
        ms = [mix[:, lanes(h)] + dot(a, s, 1, 0) for h, a, s in zip(hs, qs, ss)]
        gs = [lg[:, lanes(h)].astype(f32) for h in hs]
        square, inner = ex_own[0], ex_own[1]
        for m, g in zip(ms, gs):
            square = square + m * m
            inner = inner + g * m
        ex_own[0] = square
        ex_own[1] = inner
        for h, m in zip(hs, ms):
            mix[:, lanes(h)] = m

    for c in range(hq):
        scan_done(0, c)
        inter_forward(chunk_heads(c))

    def exchange():
        return [
            remote(
                ex_own, ex_in.at[k - 1], e_send.at[k - 1], e_recv.at[k - 1],
                {"tp": lax.rem(tp + k, n_tp)},
            )
            for k in range(1, n_tp)
        ]

    for copy in exchange():
        copy.start()
    if planes > 2:
        kv_pass(2)
    for copy in exchange():
        copy.wait_recv()
    square, inner = ex_own[0], ex_own[1]
    for k in range(n_tp - 1):
        square = square + ex_in[k, 0]
        inner = inner + ex_in[k, 1]
    features = heads * HD * n_tp
    scale = lax.rsqrt(jnp.sum(square, axis=1, keepdims=True) / features + epsilon)
    mean = scale * jnp.sum(inner, axis=1, keepdims=True) / features

    def turn(hs):
        qs = [lq[:, lanes(h)] for h in hs]
        ns = [mix[:, lanes(h)] * scale for h in hs]
        gs = [(scale * (lg[:, lanes(h)].astype(f32) - m * mean)).astype(bf16) for h, m in zip(hs, ns)]
        adj = [dot(a, g, 0, 0).astype(bf16) for a, g in zip(qs, gs)]
        for h, m, g, o in zip(hs, ns, gs, adj):
            lin_out[:, lanes(h)] = m.astype(bf16)
            gmix[:, lanes(h)] = g
            st_own[1, h] = o

    for c in range(hq):
        turn(chunk_heads(c))
        scan_start(1, c)
    for k in range(3, planes):
        kv_pass(k)

    def intra_backward(hs):
        qs = [lq[:, lanes(h)] for h in hs]
        ks = [lk[:, lanes(h)] for h in hs]
        vs = [lv[:, lanes(h)] for h in hs]
        gs = [gmix[:, lanes(h)] for h in hs]
        ss = [st_fin[0, h] for h in hs]
        ws = [scores[h] for h in hs]
        ds = [jnp.where(lower, dot(g, v, 1, 1), 0.0).astype(bf16) for g, v in zip(gs, vs)]
        gq = [dot(d, k, 1, 0) + dot(g, s, 1, 1) for d, k, g, s in zip(ds, ks, gs, ss)]
        gk = [dot(d, q, 0, 0) for d, q in zip(ds, qs)]
        gv = [dot(w, g, 0, 0) for w, g in zip(ws, gs)]
        for h, a, b, c in zip(hs, gq, gk, gv):
            grad_q[:, lanes(h)] = a.astype(bf16)
            gk_acc[:, lanes(h)] = b
            gv_acc[:, lanes(h)] = c

    for c in range(hq):
        intra_backward(chunk_heads(c))
        scan_middle(1, c)

    for copy in soft_copies((3,)):
        copy.wait_recv()

    @pl.when(last)
    def _():
        for copy in soft_copies((0, 1, 2)):
            copy.wait_recv()

    ahead = jnp.where(z < planes // 2, G, jnp.where(last, 0, 1))
    lax.fori_loop(0, ahead, query_block, 0)
    for c in range(hq):
        scan_end(1, c)
    lax.fori_loop(ahead, G, query_block, 0)
    soft_out[:, pl.ds(pl.multiple_of(p * qw, HD), qw)] = o_own[p]

    def inter_backward(hs):
        ks = [lk[:, lanes(h)] for h in hs]
        vs = [lv[:, lanes(h)] for h in hs]
        ss = [st_fin[1, h] for h in hs]
        gk = [gk_acc[:, lanes(h)] + dot(v, s, 1, 1) for h, v, s in zip(hs, vs, ss)]
        gv = [gv_acc[:, lanes(h)] + dot(k, s, 1, 0) for h, k, s in zip(hs, ks, ss)]
        for h, a, b in zip(hs, gk, gv):
            grad_k[:, lanes(h)] = a.astype(bf16)
            grad_v[:, lanes(h)] = b.astype(bf16)

    for c in range(hq):
        scan_done(1, c)
        inter_backward(chunk_heads(c))

    out_copies = [out_copy(member(d + 1), d) for d in range(G - 1)]
    for copy in out_copies:
        copy.wait_recv()
    for way in (0, 1):
        for c in range(hq):
            for copy in scan_a(way, c) + scan_c(way, c):
                copy.wait_send()
    for copy in soft_copies((0, 1, 2, 3)) + exchange() + out_copies:
        copy.wait_send()
    for k in range(1, planes):

        @pl.when(hops(k))
        def _():
            kv_hop(k).wait_send()

    for way in (0, 1):

        @pl.when(passes_on(way))
        def _():
            for c in range(hq):
                scan_z(way, c).wait_send()


def on_device(n, n_tp, lq, lk, lv, lg, sq, sk, sv, doc_start):
    length, width = lq.shape
    heads = width // HD
    hq = heads // G
    planes = n // G
    q_width = sq.shape[1]
    qw = q_width // G
    doc_row = doc_start.reshape(1, length)
    dma = pltpu.SemaphoreType.DMA
    vm = pltpu.VMEM
    span = G * length
    others = planes - 1
    kv_width = sk.shape[1]
    scratch = [
        vm((length, width), bf16), vm((length, width), bf16),
        vm((length, width), bf16), vm((length, width), bf16),
        vm((length, q_width), bf16), vm((length, kv_width), bf16), vm((length, kv_width), bf16),
        vm((8, length), jnp.int32),
        dma((7,)),
        vm((2, heads, HD, HD), bf16),
        vm((2, G, hq, HD, HD), bf16),
        vm((2, hq, HD, HD), bf16),
        vm((2, hq, HD, HD), bf16),
        vm((2, G, hq, HD, HD), bf16),
        vm((2, heads, HD, HD), bf16),
        vm((heads, length, length), bf16),
        vm((length, width), f32),
        vm((length, width), bf16),
        vm((length, width), f32),
        vm((length, width), f32),
        vm((2, length, HD), f32),
        vm((n_tp - 1, 2, length, HD), f32),
        vm((planes, 2, span, HD), bf16),
        vm((G, length, qw), bf16),
        vm((qw // HD * length, HD), bf16),
        vm((G, 8, length), jnp.int32),
        vm((G, length, qw), bf16),
        vm((1, qw), f32),
        vm((1, qw), f32),
        vm((HD, qw), f32),
        vm((HD, HD), f32),
        vm((hq, HD, HD), f32),
        dma((2, G - 1, hq)), dma((2, G - 1, hq)),
        dma((2, hq)), dma((2, hq)),
        dma((2, G - 1, hq)), dma((2, G - 1, hq)),
        dma((n_tp - 1,)), dma((n_tp - 1,)),
        dma((G - 1, 4)), dma((G - 1, 4)),
        dma((others,)), dma((others,)),
        dma((G - 1,)), dma((G - 1,)),
    ]
    hbm = pl.BlockSpec(memory_space=pl.ANY)
    here = pl.BlockSpec(memory_space=pltpu.VMEM)
    widths = [width] * 4 + [q_width]
    held = pl.pallas_call(
        functools.partial(kernel, n, n_tp),
        out_shape=[pltpu.VMEM((length, w), bf16) for w in widths],
        in_specs=[hbm] * 7 + [here],
        out_specs=[here] * 5,
        scratch_shapes=scratch,
        compiler_params=pltpu.CompilerParams(
            collective_id=0, has_side_effects=True, vmem_limit_bytes=52 * 1024 * 1024
        ),
    )(lq, lk, lv, lg, sq, sk, sv, doc_row)
    return pl.pallas_call(
        write_out,
        out_shape=[jax.ShapeDtypeStruct((length, w), bf16) for w in widths],
        in_specs=[here] * 5,
        out_specs=[hbm] * 5,
        scratch_shapes=[dma((5,))],
        compiler_params=pltpu.CompilerParams(vmem_limit_bytes=8 * 1024 * 1024),
    )(*held)


def write_out(*refs):
    sems = refs[10]
    copies = [pltpu.make_async_copy(refs[i], refs[5 + i], sems.at[i]) for i in range(5)]
    for copy in copies:
        copy.start()
    for copy in copies:
        copy.wait()


def solution(mesh):
    wide = P("ctx", "tp")
    return jax.shard_map(
        functools.partial(on_device, mesh.shape["ctx"], mesh.shape["tp"]),
        mesh=mesh,
        in_specs=(wide,) * 7 + (P("ctx"),),
        out_specs=(wide,) * 5,
        check_vma=False,
    )
```

```python
import functools
import math

import jax
import jax.numpy as jnp
from jax import lax
from jax.experimental import pallas as pl
from jax.experimental.pallas import tpu as pltpu
from jax.sharding import PartitionSpec as P

HD = 128
G = 4

MESH = pl.DeviceIdType.MESH
epsilon = 1e-06
floor_score = -1e30
f32 = jnp.float32
bf16 = jnp.bfloat16


def dot(a, b, ca, cb):
    return lax.dot_general(a, b, (((ca,), (cb,)), ((), ())), preferred_element_type=f32)


def kernel(
    n,
    n_tp,
    lq_hbm, lk_hbm, lv_hbm, lg_hbm, sq_hbm, sk_hbm, sv_hbm, doc_row,
    lin_out, grad_q, grad_k, grad_v, soft_out,
    lq, lk, lv, lg, sq, sk, sv, doc, in_sems,
    st_own, st_in, st_tot, st_z, st_out, st_fin,
    scores, mix, gmix, gk_acc, gv_acc,
    ex_own, ex_in,
    kv, q_in, q_rows, doc_in, o_own, top, total, acc, carry_ref, st_sum,
    a_send, a_recv, z_send, z_recv, c_send, c_recv,
    e_send, e_recv, s_send, s_recv, kvz_send, kvz_recv, o_send, o_recv,
):
    loads = [
        pltpu.make_async_copy(src, dst, in_sems.at[i])
        for i, (src, dst) in enumerate(
            (
                (lk_hbm, lk), (lv_hbm, lv), (lq_hbm, lq), (sk_hbm, sk),
                (sv_hbm, sv), (sq_hbm, sq), (lg_hbm, lg),
            )
        )
    ]
    for copy in loads:
        copy.start()
    length = lq.shape[0]
    heads = lq.shape[1] // HD
    hq = heads // G
    planes = n // G
    levels = planes.bit_length() - 1
    q_heads = sq.shape[1] // HD
    kv_heads = sk.shape[1] // HD
    mine = q_heads // G
    qw = mine * HD
    me = lax.axis_index("ctx")
    tp = lax.axis_index("tp")
    z = me // G
    p = lax.rem(me, G)

    def member(d):
        return lax.rem(p + d, G)

    def at_member(r):
        return {"ctx": z * G + r}

    def at_plane(zz):
        return {"ctx": zz * G + p}

    def remote(src, dst, send, recv, device):
        return pltpu.make_async_remote_copy(
            src_ref=src, dst_ref=dst, send_sem=send, recv_sem=recv,
            device_id=device, device_id_type=MESH,
        )

    barrier = pltpu.get_barrier_semaphore()
    for d in range(1, G):
        pl.semaphore_signal(barrier, inc=1, device_id=at_member(member(d)), device_id_type=MESH)
    for k in range(1, planes):
        pl.semaphore_signal(
            barrier, inc=1, device_id=at_plane(lax.rem(z + k, planes)), device_id_type=MESH
        )
    for k in range(1, n_tp):
        pl.semaphore_signal(
            barrier, inc=1, device_id={"tp": lax.rem(tp + k, n_tp)}, device_id_type=MESH
        )

    def lanes(h):
        return pl.ds(pl.multiple_of(h * HD, HD), HD)

    def chunk_heads(c):
        return [r * hq + c for r in range(G)]

    def per_chunk(body):
        for c in range(hq):
            body(chunk_heads(c))

    def per_chunk_loop(body):
        def step(c, _):
            body(chunk_heads(c))
            return 0

        lax.fori_loop(0, hq, step, 0)

    def scan_a(way, c):
        return [
            remote(
                st_own.at[way, member(d) * hq + c], st_in.at[way, p, c],
                a_send.at[way, d - 1, c], a_recv.at[way, d - 1, c], at_member(member(d)),
            )
            for d in range(1, G)
        ]

    def place(way):
        return planes - 1 - z if way else z

    def scan_z(way, level, j, c):
        return remote(
            st_tot.at[way, c], st_z.at[way, level, c],
            z_send.at[way, j, c], z_recv.at[way, level, c],
            at_plane(z - 1 - j if way else z + 1 + j),
        )

    def gives(way, level):
        half = 1 << level
        return lax.rem(place(way), 2 * half) == half - 1

    def takes(way, level):
        half = 1 << level
        return lax.rem(place(way), 2 * half) >= half

    def scan_give(way, level, c, value):
        @pl.when(gives(way, level))
        def _():
            st_tot[way, c] = value().astype(bf16)
            for j in range(1 << level):
                scan_z(way, level, j, c).start()

    def scan_c(way, c):
        return [
            remote(
                st_out.at[way, member(d), c], st_fin.at[way, p * hq + c],
                c_send.at[way, d - 1, c], c_recv.at[way, d - 1, c], at_member(member(d)),
            )
            for d in range(1, G)
        ]

    def scan_start(way, c):
        for copy in scan_a(way, c):
            copy.start()
        st_in[way, p, c] = st_own[way, p * hq + c]

    def scan_middle(way, c):
        for copy in scan_a(way, c):
            copy.wait_recv()
        parts = [st_in[way, s, c].astype(f32) for s in range(G)]
        st_sum[c] = (parts[0] + parts[1]) + (parts[2] + parts[3])

        if levels:
            scan_give(way, 0, c, lambda: st_sum[c])

    def scan_end(way, c):
        carry_ref[...] = jnp.zeros((HD, HD), f32)
        for level in range(levels):
            if level:
                scan_give(way, level, c, lambda: carry_ref[...] + st_sum[c])

            @pl.when(takes(way, level))
            def _():
                scan_z(way, level, 0, c).wait_recv()
                carry_ref[...] += st_z[way, level, c].astype(f32)

        carry = carry_ref[...]
        order = range(G - 1, -1, -1) if way else range(G)
        for s in order:
            st_out[way, s, c] = carry.astype(bf16)
            carry = carry + st_in[way, s, c].astype(f32)
        for copy in scan_c(way, c):
            copy.start()
        st_fin[way, p * hq + c] = st_out[way, p, c]

    def scan_done(way, c):
        for copy in scan_c(way, c):
            copy.wait_recv()

    loads[0].wait()
    loads[1].wait()
    doc[...] = jnp.broadcast_to(doc_row[...], doc.shape)
    for c in range(hq):
        hs = chunk_heads(c)
        outs = [dot(lk[:, lanes(h)], lv[:, lanes(h)], 0, 0).astype(bf16) for h in hs]
        for h, o in zip(hs, outs):
            st_own[0, h] = o
        if c == 0:
            pl.semaphore_wait(barrier, (G - 1) + (planes - 1) + (n_tp - 1))
        scan_start(0, c)

    def kv_lanes(r):
        return pl.ds(pl.multiple_of((r * kv_heads // G) * HD, HD), HD)

    def soft_copies(which):
        out = []
        for d in range(1, G):
            r = member(d)
            rows = pl.ds(pl.multiple_of(p * length, length), length)
            refs = (
                (sk.at[:, kv_lanes(r)], kv.at[z, 0, rows]),
                (sv.at[:, kv_lanes(r)], kv.at[z, 1, rows]),
                (doc, doc_in.at[p]),
                (sq.at[:, pl.ds(pl.multiple_of(r * qw, HD), qw)], q_in.at[p]),
            )
            for i in which:
                src, dst = refs[i]
                out.append(
                    remote(src, dst, s_send.at[d - 1, i], s_recv.at[d - 1, i], at_member(r))
                )
        return out

    for load in loads[2:6]:
        load.wait()
    own_rows = pl.ds(pl.multiple_of(p * length, length), length)
    kv[z, 0, own_rows] = sk[:, kv_lanes(p)]
    kv[z, 1, own_rows] = sv[:, kv_lanes(p)]
    doc_in[p] = doc[...]
    q_in[p] = sq[:, pl.ds(pl.multiple_of(p * qw, HD), qw)]

    lower = lax.broadcasted_iota(jnp.int32, (length, length), 0) >= lax.broadcasted_iota(
        jnp.int32, (length, length), 1
    )

    def intra_forward(hs):
        qs = [lq[:, lanes(h)] for h in hs]
        ks = [lk[:, lanes(h)] for h in hs]
        vs = [lv[:, lanes(h)] for h in hs]
        ws = [jnp.where(lower, dot(a, b, 1, 1), 0.0).astype(bf16) for a, b in zip(qs, ks)]
        ms = [dot(w, v, 1, 0) for w, v in zip(ws, vs)]
        for h, w, m in zip(hs, ws, ms):
            scores[h] = w
            mix[:, lanes(h)] = m

    last = z == planes - 1

    def soft_start(which):
        for copy in soft_copies(which):
            copy.start()

    pl.when(last)(lambda: soft_start((3,)))
    pl.when(jnp.logical_not(last))(lambda: soft_start((0, 1, 2)))
    for c in range(hq):
        intra_forward(chunk_heads(c))

    def kv_hop(k):
        block = kv.at[z - k + 1]
        return remote(block, block, kvz_send.at[k - 1], kvz_recv.at[k - 1], at_plane(z + 1))

    def kv_arrival(k):
        block = kv.at[z - k]
        return remote(block, block, kvz_send.at[k - 1], kvz_recv.at[k - 1], at_plane(z - 1))

    def hops(k):
        return (z + 1 < planes) & (z - k + 1 >= 0)

    def kv_pass(k):
        @pl.when(hops(k))
        def _():
            if k == 1:
                for copy in soft_copies((0, 1, 2)):
                    copy.wait_recv()
            else:
                kv_arrival(k - 1).wait_recv()
            kv_hop(k).start()

    span = G * length
    factor = math.log2(math.e) / math.sqrt(HD)

    def tile(b, zz, first, count):
        keys = kv[zz, 0, :count]
        vals = kv[zz, 1, :count]
        raw = dot(keys, q_rows[...], 1, 1) * factor
        row = lax.broadcasted_iota(jnp.int32, (count, qw), 0)
        begins = jnp.concatenate([doc_in[b][0:1, :]] * mine, axis=1)
        allowed = row >= begins - zz * span
        if first:
            one = lax.broadcasted_iota(jnp.int32, (1, length), 1)
            allowed = allowed & (row <= b * length + jnp.concatenate([one] * mine, axis=1))
        raw = jnp.where(allowed, raw, floor_score)
        high = jnp.max(raw, axis=0, keepdims=True)
        if not first:
            old = top[...]
            high = jnp.maximum(old, high)
            shrink = jnp.exp2(old - high)
        probs = jnp.exp2(raw - high)
        summed = jnp.sum(probs, axis=0, keepdims=True)
        update = dot(vals, probs.astype(bf16), 0, 0)
        top[...] = high
        if first:
            total[...] = summed
            acc[...] = update
        else:
            total[...] = total[...] * shrink + summed
            acc[...] = acc[...] * shrink + update

    def out_copy(b, d):
        return remote(
            o_own.at[b], soft_out.at[:, pl.ds(pl.multiple_of(p * qw, HD), qw)],
            o_send.at[d], o_recv.at[d], at_member(b),
        )

    def query_block(i, _):
        b = member(i + 1)
        for h in range(mine):
            q_rows[h * length : (h + 1) * length, :] = q_in[b, :, h * HD : (h + 1) * HD]

        @pl.when(b < G // 2)
        def _():
            tile(b, z, True, span // 2)

        @pl.when(b >= G // 2)
        def _():
            tile(b, z, True, span)

        def earlier_plane(k, _):
            @pl.when((i == 0) & jnp.logical_not(hops(k + 1)))
            def _():
                kv_arrival(k).wait_recv()

            tile(b, z - k, False, span)
            return 0

        lax.fori_loop(1, z + 1, earlier_plane, 0)
        out = acc[...] / total[...]
        for h in range(mine):
            o_own[b, :, h * HD : (h + 1) * HD] = jnp.transpose(
                out[:, h * length : (h + 1) * length]
            ).astype(bf16)

        @pl.when(i < G - 1)
        def _():
            out_copy(b, i).start()

        return 0

    for c in range(hq):
        scan_middle(0, c)
    for c in range(hq):
        scan_end(0, c)
    pl.when(last)(lambda: soft_start((0, 1, 2)))
    pl.when(jnp.logical_not(last))(lambda: soft_start((3,)))
    kv_pass(1)
    loads[6].wait()

    ex_own[...] = jnp.zeros_like(ex_own)

    def inter_forward(hs):
        qs = [lq[:, lanes(h)] for h in hs]
        ss = [st_fin[0, h] for h in hs]
        ms = [mix[:, lanes(h)] + dot(a, s, 1, 0) for h, a, s in zip(hs, qs, ss)]
        gs = [lg[:, lanes(h)].astype(f32) for h in hs]
        square, inner = ex_own[0], ex_own[1]
        for m, g in zip(ms, gs):
            square = square + m * m
            inner = inner + g * m
        ex_own[0] = square
        ex_own[1] = inner
        for h, m in zip(hs, ms):
            mix[:, lanes(h)] = m

    for c in range(hq):
        scan_done(0, c)
        inter_forward(chunk_heads(c))

    def exchange():
        return [
            remote(
                ex_own, ex_in.at[k - 1], e_send.at[k - 1], e_recv.at[k - 1],
                {"tp": lax.rem(tp + k, n_tp)},
            )
            for k in range(1, n_tp)
        ]

    for copy in exchange():
        copy.start()
    if planes > 2:
        kv_pass(2)
    for copy in exchange():
        copy.wait_recv()
    square, inner = ex_own[0], ex_own[1]
    for k in range(n_tp - 1):
        square = square + ex_in[k, 0]
        inner = inner + ex_in[k, 1]
    features = heads * HD * n_tp
    scale = lax.rsqrt(jnp.sum(square, axis=1, keepdims=True) / features + epsilon)
    mean = scale * jnp.sum(inner, axis=1, keepdims=True) / features

    def turn(hs):
        qs = [lq[:, lanes(h)] for h in hs]
        ns = [mix[:, lanes(h)] * scale for h in hs]
        gs = [(scale * (lg[:, lanes(h)].astype(f32) - m * mean)).astype(bf16) for h, m in zip(hs, ns)]
        adj = [dot(a, g, 0, 0).astype(bf16) for a, g in zip(qs, gs)]
        for h, m, g, o in zip(hs, ns, gs, adj):
            lin_out[:, lanes(h)] = m.astype(bf16)
            gmix[:, lanes(h)] = g
            st_own[1, h] = o

    for c in range(hq):
        turn(chunk_heads(c))
        scan_start(1, c)
    for k in range(3, planes):
        kv_pass(k)

    def intra_backward(hs):
        qs = [lq[:, lanes(h)] for h in hs]
        ks = [lk[:, lanes(h)] for h in hs]
        vs = [lv[:, lanes(h)] for h in hs]
        gs = [gmix[:, lanes(h)] for h in hs]
        ss = [st_fin[0, h] for h in hs]
        ws = [scores[h] for h in hs]
        ds = [jnp.where(lower, dot(g, v, 1, 1), 0.0).astype(bf16) for g, v in zip(gs, vs)]
        gq = [dot(d, k, 1, 0) + dot(g, s, 1, 1) for d, k, g, s in zip(ds, ks, gs, ss)]
        gk = [dot(d, q, 0, 0) for d, q in zip(ds, qs)]
        gv = [dot(w, g, 0, 0) for w, g in zip(ws, gs)]
        for h, a, b, c in zip(hs, gq, gk, gv):
            grad_q[:, lanes(h)] = a.astype(bf16)
            gk_acc[:, lanes(h)] = b
            gv_acc[:, lanes(h)] = c

    for c in range(hq):
        if c % 2 == 0:
            intra_backward(chunk_heads(c // 2))
        scan_middle(1, c)
    for c in range((hq + 1) // 2, hq):
        intra_backward(chunk_heads(c))

    for copy in soft_copies((3,)):
        copy.wait_recv()

    @pl.when(last)
    def _():
        for copy in soft_copies((0, 1, 2)):
            copy.wait_recv()

    ahead = jnp.where(z < planes // 2, G // 2, 0)
    lax.fori_loop(0, ahead, query_block, 0)
    for c in range(hq):
        scan_end(1, c)
    lax.fori_loop(ahead, G, query_block, 0)
    soft_out[:, pl.ds(pl.multiple_of(p * qw, HD), qw)] = o_own[p]

    def inter_backward(hs):
        ks = [lk[:, lanes(h)] for h in hs]
        vs = [lv[:, lanes(h)] for h in hs]
        ss = [st_fin[1, h] for h in hs]
        gk = [gk_acc[:, lanes(h)] + dot(v, s, 1, 1) for h, v, s in zip(hs, vs, ss)]
        gv = [gv_acc[:, lanes(h)] + dot(k, s, 1, 0) for h, k, s in zip(hs, ks, ss)]
        for h, a, b in zip(hs, gk, gv):
            grad_k[:, lanes(h)] = a.astype(bf16)
            grad_v[:, lanes(h)] = b.astype(bf16)

    for c in range(hq):
        scan_done(1, c)
        inter_backward(chunk_heads(c))

    out_copies = [out_copy(member(d + 1), d) for d in range(G - 1)]
    for copy in out_copies:
        copy.wait_recv()
    for way in (0, 1):
        for c in range(hq):
            for copy in scan_a(way, c) + scan_c(way, c):
                copy.wait_send()
    for copy in soft_copies((0, 1, 2, 3)) + exchange() + out_copies:
        copy.wait_send()
    for k in range(1, planes):

        @pl.when(hops(k))
        def _():
            kv_hop(k).wait_send()

    for way in (0, 1):

        for level in range(levels):

            @pl.when(gives(way, level))
            def _():
                for c in range(hq):
                    for j in range(1 << level):
                        scan_z(way, level, j, c).wait_send()


def on_device(n, n_tp, lq, lk, lv, lg, sq, sk, sv, doc_start):
    length, width = lq.shape
    heads = width // HD
    hq = heads // G
    planes = n // G
    q_width = sq.shape[1]
    qw = q_width // G
    doc_row = doc_start.reshape(1, length)
    dma = pltpu.SemaphoreType.DMA
    vm = pltpu.VMEM
    span = G * length
    others = planes - 1
    levels = planes.bit_length() - 1
    kv_width = sk.shape[1]
    scratch = [
        vm((length, width), bf16), vm((length, width), bf16),
        vm((length, width), bf16), vm((length, width), bf16),
        vm((length, q_width), bf16), vm((length, kv_width), bf16), vm((length, kv_width), bf16),
        vm((8, length), jnp.int32),
        dma((7,)),
        vm((2, heads, HD, HD), bf16),
        vm((2, G, hq, HD, HD), bf16),
        vm((2, hq, HD, HD), bf16),
        vm((2, levels, hq, HD, HD), bf16),
        vm((2, G, hq, HD, HD), bf16),
        vm((2, heads, HD, HD), bf16),
        vm((heads, length, length), bf16),
        vm((length, width), f32),
        vm((length, width), bf16),
        vm((length, width), f32),
        vm((length, width), f32),
        vm((2, length, HD), f32),
        vm((n_tp - 1, 2, length, HD), f32),
        vm((planes, 2, span, HD), bf16),
        vm((G, length, qw), bf16),
        vm((qw // HD * length, HD), bf16),
        vm((G, 8, length), jnp.int32),
        vm((G, length, qw), bf16),
        vm((1, qw), f32),
        vm((1, qw), f32),
        vm((HD, qw), f32),
        vm((HD, HD), f32),
        vm((hq, HD, HD), f32),
        dma((2, G - 1, hq)), dma((2, G - 1, hq)),
        dma((2, planes // 2, hq)), dma((2, levels, hq)),
        dma((2, G - 1, hq)), dma((2, G - 1, hq)),
        dma((n_tp - 1,)), dma((n_tp - 1,)),
        dma((G - 1, 4)), dma((G - 1, 4)),
        dma((others,)), dma((others,)),
        dma((G - 1,)), dma((G - 1,)),
    ]
    hbm = pl.BlockSpec(memory_space=pl.ANY)
    here = pl.BlockSpec(memory_space=pltpu.VMEM)
    widths = [width] * 4 + [q_width]
    held = pl.pallas_call(
        functools.partial(kernel, n, n_tp),
        out_shape=[pltpu.VMEM((length, w), bf16) for w in widths],
        in_specs=[hbm] * 7 + [here],
        out_specs=[here] * 5,
        scratch_shapes=scratch,
        compiler_params=pltpu.CompilerParams(
            collective_id=0, has_side_effects=True, vmem_limit_bytes=52 * 1024 * 1024
        ),
    )(lq, lk, lv, lg, sq, sk, sv, doc_row)
    return pl.pallas_call(
        write_out,
        out_shape=[jax.ShapeDtypeStruct((length, w), bf16) for w in widths],
        in_specs=[here] * 5,
        out_specs=[hbm] * 5,
        scratch_shapes=[dma((5,))],
        compiler_params=pltpu.CompilerParams(vmem_limit_bytes=8 * 1024 * 1024),
    )(*held)


def write_out(*refs):
    sems = refs[10]
    copies = [pltpu.make_async_copy(refs[i], refs[5 + i], sems.at[i]) for i in range(5)]
    for copy in copies:
        copy.start()
    for copy in copies:
        copy.wait()


def solution(mesh):
    wide = P("ctx", "tp")
    return jax.shard_map(
        functools.partial(on_device, mesh.shape["ctx"], mesh.shape["tp"]),
        mesh=mesh,
        in_specs=(wide,) * 7 + (P("ctx"),),
        out_specs=(wide,) * 5,
        check_vma=False,
    )
```

```python
import functools
import math

import jax
import jax.numpy as jnp
from jax import lax
from jax.experimental import pallas as pl
from jax.experimental.pallas import tpu as pltpu
from jax.sharding import PartitionSpec as P

HD = 128
G = 4

MESH = pl.DeviceIdType.MESH
epsilon = 1e-06
floor_score = -1e30
f32 = jnp.float32
bf16 = jnp.bfloat16


def dot(a, b, ca, cb):
    return lax.dot_general(a, b, (((ca,), (cb,)), ((), ())), preferred_element_type=f32)


def kernel(
    n,
    n_tp,
    lq_hbm, lk_hbm, lv_hbm, lg_hbm, sq_hbm, sk_hbm, sv_hbm, doc_row,
    lin_out, grad_q, grad_k, grad_v, soft_out,
    lq, lk, lv, lg, sq, sk, sv, doc, in_sems,
    st_own, st_in, st_tot, st_z, st_out, st_fin,
    scores, mix, gmix, gk_acc, gv_acc,
    ex_own, ex_in,
    kv, q_in, q_rows, doc_in, o_own, top, total, acc, carry_ref, st_sum,
    a_send, a_recv, z_send, z_recv, c_send, c_recv,
    e_send, e_recv, s_send, s_recv, kvz_send, kvz_recv, o_send, o_recv,
):
    loads = [
        pltpu.make_async_copy(src, dst, in_sems.at[i])
        for i, (src, dst) in enumerate(
            (
                (lk_hbm, lk), (lv_hbm, lv), (lq_hbm, lq), (sk_hbm, sk),
                (sv_hbm, sv), (sq_hbm, sq), (lg_hbm, lg),
            )
        )
    ]
    for copy in loads:
        copy.start()
    length = lq.shape[0]
    heads = lq.shape[1] // HD
    hq = heads // G
    planes = n // G
    q_heads = sq.shape[1] // HD
    kv_heads = sk.shape[1] // HD
    mine = q_heads // G
    qw = mine * HD
    me = lax.axis_index("ctx")
    tp = lax.axis_index("tp")
    z = me // G
    p = lax.rem(me, G)

    def member(d):
        return lax.rem(p + d, G)

    def at_member(r):
        return {"ctx": z * G + r}

    def at_plane(zz):
        return {"ctx": zz * G + p}

    def remote(src, dst, send, recv, device):
        return pltpu.make_async_remote_copy(
            src_ref=src, dst_ref=dst, send_sem=send, recv_sem=recv,
            device_id=device, device_id_type=MESH,
        )

    barrier = pltpu.get_barrier_semaphore()
    for d in range(1, G):
        pl.semaphore_signal(barrier, inc=1, device_id=at_member(member(d)), device_id_type=MESH)
    for k in range(1, planes):
        pl.semaphore_signal(
            barrier, inc=1, device_id=at_plane(lax.rem(z + k, planes)), device_id_type=MESH
        )
    for k in range(1, n_tp):
        pl.semaphore_signal(
            barrier, inc=1, device_id={"tp": lax.rem(tp + k, n_tp)}, device_id_type=MESH
        )

    def lanes(h):
        return pl.ds(pl.multiple_of(h * HD, HD), HD)

    def chunk_heads(c):
        return [r * hq + c for r in range(G)]

    def per_chunk(body):
        for c in range(hq):
            body(chunk_heads(c))

    def per_chunk_loop(body):
        def step(c, _):
            body(chunk_heads(c))
            return 0

        lax.fori_loop(0, hq, step, 0)

    def scan_a(way, c):
        return [
            remote(
                st_own.at[way, member(d) * hq + c], st_in.at[way, p, c],
                a_send.at[way, d - 1, c], a_recv.at[way, d - 1, c], at_member(member(d)),
            )
            for d in range(1, G)
        ]

    def scan_z(way, c):
        return remote(
            st_tot.at[way, c], st_z.at[way, c], z_send.at[way, c], z_recv.at[way, c],
            at_plane(z - 1 if way else z + 1),
        )

    def passes_on(way):
        return z > 0 if way else z + 1 < planes

    def is_passed(way):
        return passes_on(1 - way)

    def scan_c(way, c):
        return [
            remote(
                st_out.at[way, member(d), c], st_fin.at[way, p * hq + c],
                c_send.at[way, d - 1, c], c_recv.at[way, d - 1, c], at_member(member(d)),
            )
            for d in range(1, G)
        ]

    def scan_start(way, c):
        for copy in scan_a(way, c):
            copy.start()
        st_in[way, p, c] = st_own[way, p * hq + c]

    def scan_middle(way, c):
        for copy in scan_a(way, c):
            copy.wait_recv()
        parts = [st_in[way, s, c].astype(f32) for s in range(G)]
        st_sum[c] = (parts[0] + parts[1]) + (parts[2] + parts[3])

        @pl.when(passes_on(way) & jnp.logical_not(is_passed(way)))
        def _():
            st_tot[way, c] = st_sum[c].astype(bf16)
            scan_z(way, c).start()

    def scan_end(way, c):
        carry_ref[...] = jnp.zeros((HD, HD), f32)

        @pl.when(is_passed(way))
        def _():
            scan_z(way, c).wait_recv()
            carry_ref[...] = st_z[way, c].astype(f32)

        @pl.when(is_passed(way) & passes_on(way))
        def _():
            st_tot[way, c] = (carry_ref[...] + st_sum[c]).astype(bf16)
            scan_z(way, c).start()

        carry = carry_ref[...]
        order = range(G - 1, -1, -1) if way else range(G)
        for s in order:
            st_out[way, s, c] = carry.astype(bf16)
            carry = carry + st_in[way, s, c].astype(f32)
        for copy in scan_c(way, c):
            copy.start()
        st_fin[way, p * hq + c] = st_out[way, p, c]

    def scan_done(way, c):
        for copy in scan_c(way, c):
            copy.wait_recv()

    loads[0].wait()
    loads[1].wait()
    doc[...] = jnp.broadcast_to(doc_row[...], doc.shape)
    for c in range(hq):
        hs = chunk_heads(c)
        outs = [dot(lk[:, lanes(h)], lv[:, lanes(h)], 0, 0).astype(bf16) for h in hs]
        for h, o in zip(hs, outs):
            st_own[0, h] = o
        if c == 0:
            pl.semaphore_wait(barrier, (G - 1) + (planes - 1) + (n_tp - 1))
        scan_start(0, c)

    def kv_lanes(r):
        return pl.ds(pl.multiple_of((r * kv_heads // G) * HD, HD), HD)

    def soft_copies(which):
        out = []
        for d in range(1, G):
            r = member(d)
            rows = pl.ds(pl.multiple_of(p * length, length), length)
            refs = (
                (sk.at[:, kv_lanes(r)], kv.at[z, 0, rows]),
                (sv.at[:, kv_lanes(r)], kv.at[z, 1, rows]),
                (doc, doc_in.at[p]),
                (sq.at[:, pl.ds(pl.multiple_of(r * qw, HD), qw)], q_in.at[p]),
            )
            for i in which:
                src, dst = refs[i]
                out.append(
                    remote(src, dst, s_send.at[d - 1, i], s_recv.at[d - 1, i], at_member(r))
                )
        return out

    for load in loads[2:6]:
        load.wait()
    own_rows = pl.ds(pl.multiple_of(p * length, length), length)
    kv[z, 0, own_rows] = sk[:, kv_lanes(p)]
    kv[z, 1, own_rows] = sv[:, kv_lanes(p)]
    doc_in[p] = doc[...]
    q_in[p] = sq[:, pl.ds(pl.multiple_of(p * qw, HD), qw)]

    lower = lax.broadcasted_iota(jnp.int32, (length, length), 0) >= lax.broadcasted_iota(
        jnp.int32, (length, length), 1
    )

    def intra_forward(hs):
        qs = [lq[:, lanes(h)] for h in hs]
        ks = [lk[:, lanes(h)] for h in hs]
        vs = [lv[:, lanes(h)] for h in hs]
        ws = [jnp.where(lower, dot(a, b, 1, 1), 0.0).astype(bf16) for a, b in zip(qs, ks)]
        ms = [dot(w, v, 1, 0) for w, v in zip(ws, vs)]
        for h, w, m in zip(hs, ws, ms):
            scores[h] = w
            mix[:, lanes(h)] = m

    last = z == planes - 1

    def soft_start(which):
        for copy in soft_copies(which):
            copy.start()

    pl.when(last)(lambda: soft_start((3,)))
    pl.when(jnp.logical_not(last))(lambda: soft_start((0, 1, 2)))
    for c in range(hq):
        intra_forward(chunk_heads(c))

    def kv_copy(k):
        return remote(
            kv.at[z], kv.at[z], kvz_send.at[k - 1], kvz_recv.at[k - 1], at_plane(z + k)
        )

    def kv_arrival(k):
        block = kv.at[z - k]
        return remote(block, block, kvz_send.at[k - 1], kvz_recv.at[k - 1], at_plane(z - k))

    def kv_pass(k):
        @pl.when(z + k < planes)
        def _():
            if k == 1:
                for copy in soft_copies((0, 1, 2)):
                    copy.wait_recv()
            kv_copy(k).start()

    span = G * length
    factor = math.log2(math.e) / math.sqrt(HD)

    def tile(b, zz, first, count):
        keys = kv[zz, 0, :count]
        vals = kv[zz, 1, :count]
        raw = dot(keys, q_rows[...], 1, 1) * factor
        row = lax.broadcasted_iota(jnp.int32, (count, qw), 0)
        begins = jnp.concatenate([doc_in[b][0:1, :]] * mine, axis=1)
        allowed = row >= begins - zz * span
        if first:
            one = lax.broadcasted_iota(jnp.int32, (1, length), 1)
            allowed = allowed & (row <= b * length + jnp.concatenate([one] * mine, axis=1))
        raw = jnp.where(allowed, raw, floor_score)
        high = jnp.max(raw, axis=0, keepdims=True)
        if not first:
            old = top[...]
            high = jnp.maximum(old, high)
            shrink = jnp.exp2(old - high)
        probs = jnp.exp2(raw - high)
        summed = jnp.sum(probs, axis=0, keepdims=True)
        update = dot(vals, probs.astype(bf16), 0, 0)
        top[...] = high
        if first:
            total[...] = summed
            acc[...] = update
        else:
            total[...] = total[...] * shrink + summed
            acc[...] = acc[...] * shrink + update

    def out_copy(b, d):
        return remote(
            o_own.at[b], soft_out.at[:, pl.ds(pl.multiple_of(p * qw, HD), qw)],
            o_send.at[d], o_recv.at[d], at_member(b),
        )

    def query_block(i, _):
        b = member(i + 1)
        for h in range(mine):
            q_rows[h * length : (h + 1) * length, :] = q_in[b, :, h * HD : (h + 1) * HD]

        @pl.when(b < G // 2)
        def _():
            tile(b, z, True, span // 2)

        @pl.when(b >= G // 2)
        def _():
            tile(b, z, True, span)

        def earlier_plane(k, _):
            @pl.when(i == 0)
            def _():
                kv_arrival(k).wait_recv()

            tile(b, z - k, False, span)
            return 0

        lax.fori_loop(1, z + 1, earlier_plane, 0)
        out = acc[...] / total[...]
        for h in range(mine):
            o_own[b, :, h * HD : (h + 1) * HD] = jnp.transpose(
                out[:, h * length : (h + 1) * length]
            ).astype(bf16)

        @pl.when(i < G - 1)
        def _():
            out_copy(b, i).start()

        return 0

    for c in range(hq):
        scan_middle(0, c)
        scan_end(0, c)
    pl.when(last)(lambda: soft_start((0, 1, 2)))
    pl.when(jnp.logical_not(last))(lambda: soft_start((3,)))
    kv_pass(1)
    loads[6].wait()

    ex_own[...] = jnp.zeros_like(ex_own)

    def inter_forward(hs):
        qs = [lq[:, lanes(h)] for h in hs]
        ss = [st_fin[0, h] for h in hs]
        ms = [mix[:, lanes(h)] + dot(a, s, 1, 0) for h, a, s in zip(hs, qs, ss)]
        gs = [lg[:, lanes(h)].astype(f32) for h in hs]
        square, inner = ex_own[0], ex_own[1]
        for m, g in zip(ms, gs):
            square = square + m * m
            inner = inner + g * m
        ex_own[0] = square
        ex_own[1] = inner
        for h, m in zip(hs, ms):
            mix[:, lanes(h)] = m

    for c in range(hq):
        scan_done(0, c)
        inter_forward(chunk_heads(c))

    def exchange():
        return [
            remote(
                ex_own, ex_in.at[k - 1], e_send.at[k - 1], e_recv.at[k - 1],
                {"tp": lax.rem(tp + k, n_tp)},
            )
            for k in range(1, n_tp)
        ]

    for copy in exchange():
        copy.start()
    for k in range(2, planes):
        kv_pass(k)
    for copy in exchange():
        copy.wait_recv()
    square, inner = ex_own[0], ex_own[1]
    for k in range(n_tp - 1):
        square = square + ex_in[k, 0]
        inner = inner + ex_in[k, 1]
    features = heads * HD * n_tp
    scale = lax.rsqrt(jnp.sum(square, axis=1, keepdims=True) / features + epsilon)
    mean = scale * jnp.sum(inner, axis=1, keepdims=True) / features

    def turn(hs):
        qs = [lq[:, lanes(h)] for h in hs]
        ns = [mix[:, lanes(h)] * scale for h in hs]
        gs = [(scale * (lg[:, lanes(h)].astype(f32) - m * mean)).astype(bf16) for h, m in zip(hs, ns)]
        adj = [dot(a, g, 0, 0).astype(bf16) for a, g in zip(qs, gs)]
        for h, m, g, o in zip(hs, ns, gs, adj):
            lin_out[:, lanes(h)] = m.astype(bf16)
            gmix[:, lanes(h)] = g
            st_own[1, h] = o

    for c in range(hq):
        turn(chunk_heads(c))
        scan_start(1, c)

    def intra_backward(hs):
        qs = [lq[:, lanes(h)] for h in hs]
        ks = [lk[:, lanes(h)] for h in hs]
        vs = [lv[:, lanes(h)] for h in hs]
        gs = [gmix[:, lanes(h)] for h in hs]
        ss = [st_fin[0, h] for h in hs]
        ws = [scores[h] for h in hs]
        ds = [jnp.where(lower, dot(g, v, 1, 1), 0.0).astype(bf16) for g, v in zip(gs, vs)]
        gq = [dot(d, k, 1, 0) + dot(g, s, 1, 1) for d, k, g, s in zip(ds, ks, gs, ss)]
        gk = [dot(d, q, 0, 0) for d, q in zip(ds, qs)]
        gv = [dot(w, g, 0, 0) for w, g in zip(ws, gs)]
        for h, a, b, c in zip(hs, gq, gk, gv):
            grad_q[:, lanes(h)] = a.astype(bf16)
            gk_acc[:, lanes(h)] = b
            gv_acc[:, lanes(h)] = c

    for c in range(hq):
        if c % 2 == 0:
            intra_backward(chunk_heads(c // 2))
        scan_middle(1, c)
    rest = list(range((hq + 1) // 2, hq))
    for c in rest[:1]:
        intra_backward(chunk_heads(c))

    for copy in soft_copies((3,)):
        copy.wait_recv()

    @pl.when(last)
    def _():
        for copy in soft_copies((0, 1, 2)):
            copy.wait_recv()

    ahead = jnp.where(z == 0, G, jnp.where(z < planes // 2, G // 2, 0))
    lax.fori_loop(0, ahead, query_block, 0)
    for c in range(hq):
        scan_end(1, c)
    for c in rest[1:]:
        intra_backward(chunk_heads(c))
    lax.fori_loop(ahead, G, query_block, 0)
    soft_out[:, pl.ds(pl.multiple_of(p * qw, HD), qw)] = o_own[p]

    def inter_backward(hs):
        ks = [lk[:, lanes(h)] for h in hs]
        vs = [lv[:, lanes(h)] for h in hs]
        ss = [st_fin[1, h] for h in hs]
        gk = [gk_acc[:, lanes(h)] + dot(v, s, 1, 1) for h, v, s in zip(hs, vs, ss)]
        gv = [gv_acc[:, lanes(h)] + dot(k, s, 1, 0) for h, k, s in zip(hs, ks, ss)]
        for h, a, b in zip(hs, gk, gv):
            grad_k[:, lanes(h)] = a.astype(bf16)
            grad_v[:, lanes(h)] = b.astype(bf16)

    for c in range(hq):
        scan_done(1, c)
        inter_backward(chunk_heads(c))

    out_copies = [out_copy(member(d + 1), d) for d in range(G - 1)]
    for copy in out_copies:
        copy.wait_recv()
    for way in (0, 1):
        for c in range(hq):
            for copy in scan_a(way, c) + scan_c(way, c):
                copy.wait_send()
    for copy in soft_copies((0, 1, 2, 3)) + exchange() + out_copies:
        copy.wait_send()
    for k in range(1, planes):

        @pl.when(z + k < planes)
        def _():
            kv_copy(k).wait_send()

    for way in (0, 1):

        @pl.when(passes_on(way))
        def _():
            for c in range(hq):
                scan_z(way, c).wait_send()


def on_device(n, n_tp, lq, lk, lv, lg, sq, sk, sv, doc_start):
    length, width = lq.shape
    heads = width // HD
    hq = heads // G
    planes = n // G
    q_width = sq.shape[1]
    qw = q_width // G
    doc_row = doc_start.reshape(1, length)
    dma = pltpu.SemaphoreType.DMA
    vm = pltpu.VMEM
    span = G * length
    others = planes - 1
    kv_width = sk.shape[1]
    scratch = [
        vm((length, width), bf16), vm((length, width), bf16),
        vm((length, width), bf16), vm((length, width), bf16),
        vm((length, q_width), bf16), vm((length, kv_width), bf16), vm((length, kv_width), bf16),
        vm((8, length), jnp.int32),
        dma((7,)),
        vm((2, heads, HD, HD), bf16),
        vm((2, G, hq, HD, HD), bf16),
        vm((2, hq, HD, HD), bf16),
        vm((2, hq, HD, HD), bf16),
        vm((2, G, hq, HD, HD), bf16),
        vm((2, heads, HD, HD), bf16),
        vm((heads, length, length), bf16),
        vm((length, width), f32),
        vm((length, width), bf16),
        vm((length, width), f32),
        vm((length, width), f32),
        vm((2, length, HD), f32),
        vm((n_tp - 1, 2, length, HD), f32),
        vm((planes, 2, span, HD), bf16),
        vm((G, length, qw), bf16),
        vm((qw // HD * length, HD), bf16),
        vm((G, 8, length), jnp.int32),
        vm((G, length, qw), bf16),
        vm((1, qw), f32),
        vm((1, qw), f32),
        vm((HD, qw), f32),
        vm((HD, HD), f32),
        vm((hq, HD, HD), f32),
        dma((2, G - 1, hq)), dma((2, G - 1, hq)),
        dma((2, hq)), dma((2, hq)),
        dma((2, G - 1, hq)), dma((2, G - 1, hq)),
        dma((n_tp - 1,)), dma((n_tp - 1,)),
        dma((G - 1, 4)), dma((G - 1, 4)),
        dma((others,)), dma((others,)),
        dma((G - 1,)), dma((G - 1,)),
    ]
    hbm = pl.BlockSpec(memory_space=pl.ANY)
    here = pl.BlockSpec(memory_space=pltpu.VMEM)
    widths = [width] * 4 + [q_width]
    held = pl.pallas_call(
        functools.partial(kernel, n, n_tp),
        out_shape=[pltpu.VMEM((length, w), bf16) for w in widths],
        in_specs=[hbm] * 7 + [here],
        out_specs=[here] * 5,
        scratch_shapes=scratch,
        compiler_params=pltpu.CompilerParams(
            collective_id=0, has_side_effects=True, vmem_limit_bytes=52 * 1024 * 1024
        ),
    )(lq, lk, lv, lg, sq, sk, sv, doc_row)
    return pl.pallas_call(
        write_out,
        out_shape=[jax.ShapeDtypeStruct((length, w), bf16) for w in widths],
        in_specs=[here] * 5,
        out_specs=[hbm] * 5,
        scratch_shapes=[dma((5,))],
        compiler_params=pltpu.CompilerParams(vmem_limit_bytes=8 * 1024 * 1024),
    )(*held)


def write_out(*refs):
    sems = refs[10]
    copies = [pltpu.make_async_copy(refs[i], refs[5 + i], sems.at[i]) for i in range(5)]
    for copy in copies:
        copy.start()
    for copy in copies:
        copy.wait()


def solution(mesh):
    wide = P("ctx", "tp")
    return jax.shard_map(
        functools.partial(on_device, mesh.shape["ctx"], mesh.shape["tp"]),
        mesh=mesh,
        in_specs=(wide,) * 7 + (P("ctx"),),
        out_specs=(wide,) * 5,
        check_vma=False,
    )
```

```python
import functools
import math

import jax
import jax.numpy as jnp
from jax import lax
from jax.experimental import pallas as pl
from jax.experimental.pallas import tpu as pltpu
from jax.sharding import PartitionSpec as P

HD = 128
G = 4

MESH = pl.DeviceIdType.MESH
epsilon = 1e-06
floor_score = -1e30
f32 = jnp.float32
bf16 = jnp.bfloat16


def dot(a, b, ca, cb):
    return lax.dot_general(a, b, (((ca,), (cb,)), ((), ())), preferred_element_type=f32)


def kernel(
    n,
    n_tp,
    lq_hbm, lk_hbm, lv_hbm, lg_hbm, sq_hbm, sk_hbm, sv_hbm, doc_row,
    lin_out, grad_q, grad_k, grad_v, soft_out,
    lq, lk, lv, lg, sq, sk, sv, doc, in_sems,
    st_own, st_in, st_tot, st_z, st_out, st_fin,
    scores, mix, gmix, gk_acc, gv_acc,
    ex_own, ex_in,
    kv, q_in, q_rows, doc_in, o_own, top, total, acc, carry_ref, st_sum,
    a_send, a_recv, z_send, z_recv, c_send, c_recv,
    e_send, e_recv, s_send, s_recv, kvz_send, kvz_recv, o_send, o_recv,
):
    loads = [
        pltpu.make_async_copy(src, dst, in_sems.at[i])
        for i, (src, dst) in enumerate(
            (
                (lk_hbm, lk), (lv_hbm, lv), (lq_hbm, lq), (sk_hbm, sk),
                (sv_hbm, sv), (sq_hbm, sq), (lg_hbm, lg),
            )
        )
    ]
    for copy in loads:
        copy.start()
    length = lq.shape[0]
    heads = lq.shape[1] // HD
    hq = heads // G
    planes = n // G
    q_heads = sq.shape[1] // HD
    kv_heads = sk.shape[1] // HD
    mine = q_heads // G
    qw = mine * HD
    me = lax.axis_index("ctx")
    tp = lax.axis_index("tp")
    z = me // G
    p = lax.rem(me, G)

    def member(d):
        return lax.rem(p + d, G)

    def at_member(r):
        return {"ctx": z * G + r}

    def at_plane(zz):
        return {"ctx": zz * G + p}

    def remote(src, dst, send, recv, device):
        return pltpu.make_async_remote_copy(
            src_ref=src, dst_ref=dst, send_sem=send, recv_sem=recv,
            device_id=device, device_id_type=MESH,
        )

    barrier = pltpu.get_barrier_semaphore()
    for d in range(1, G):
        pl.semaphore_signal(barrier, inc=1, device_id=at_member(member(d)), device_id_type=MESH)
    for step, there in ((1, z + 1 < planes), (-1, z > 0)):

        @pl.when(there)
        def _():
            pl.semaphore_signal(
                barrier, inc=1, device_id=at_plane(z + step), device_id_type=MESH
            )

    for k in range(1, n_tp):
        pl.semaphore_signal(
            barrier, inc=1, device_id={"tp": lax.rem(tp + k, n_tp)}, device_id_type=MESH
        )

    def lanes(h):
        return pl.ds(pl.multiple_of(h * HD, HD), HD)

    def chunk_heads(c):
        return [r * hq + c for r in range(G)]

    def per_chunk(body):
        for c in range(hq):
            body(chunk_heads(c))

    def per_chunk_loop(body):
        def step(c, _):
            body(chunk_heads(c))
            return 0

        lax.fori_loop(0, hq, step, 0)

    def scan_a(way, c):
        return [
            remote(
                st_own.at[way, member(d) * hq + c], st_in.at[way, p, c],
                a_send.at[way, d - 1, c], a_recv.at[way, d - 1, c], at_member(member(d)),
            )
            for d in range(1, G)
        ]

    def scan_z(way, c):
        return remote(
            st_tot.at[way, c], st_z.at[way, c], z_send.at[way, c], z_recv.at[way, c],
            at_plane(z - 1 if way else z + 1),
        )

    def passes_on(way):
        return z > 0 if way else z + 1 < planes

    def is_passed(way):
        return passes_on(1 - way)

    def scan_c(way, c):
        return [
            remote(
                st_out.at[way, member(d), c], st_fin.at[way, p * hq + c],
                c_send.at[way, d - 1, c], c_recv.at[way, d - 1, c], at_member(member(d)),
            )
            for d in range(1, G)
        ]

    def scan_start(way, c):
        for copy in scan_a(way, c):
            copy.start()
        st_in[way, p, c] = st_own[way, p * hq + c]

    def scan_middle(way, c):
        for copy in scan_a(way, c):
            copy.wait_recv()
        parts = [st_in[way, s, c].astype(f32) for s in range(G)]
        st_sum[c] = (parts[0] + parts[1]) + (parts[2] + parts[3])

        @pl.when(passes_on(way) & jnp.logical_not(is_passed(way)))
        def _():
            st_tot[way, c] = st_sum[c].astype(bf16)
            scan_z(way, c).start()

    def scan_end(way, c):
        carry_ref[...] = jnp.zeros((HD, HD), f32)

        @pl.when(is_passed(way))
        def _():
            scan_z(way, c).wait_recv()
            carry_ref[...] = st_z[way, c].astype(f32)

        @pl.when(is_passed(way) & passes_on(way))
        def _():
            st_tot[way, c] = (carry_ref[...] + st_sum[c]).astype(bf16)
            scan_z(way, c).start()

        carry = carry_ref[...]
        order = range(G - 1, -1, -1) if way else range(G)
        for s in order:
            st_out[way, s, c] = carry.astype(bf16)
            carry = carry + st_in[way, s, c].astype(f32)
        for copy in scan_c(way, c):
            copy.start()
        st_fin[way, p * hq + c] = st_out[way, p, c]

    def scan_done(way, c):
        for copy in scan_c(way, c):
            copy.wait_recv()

    loads[0].wait()
    loads[1].wait()
    doc[...] = jnp.broadcast_to(doc_row[...], doc.shape)
    for c in range(hq):
        hs = chunk_heads(c)
        outs = [dot(lk[:, lanes(h)], lv[:, lanes(h)], 0, 0).astype(bf16) for h in hs]
        for h, o in zip(hs, outs):
            st_own[0, h] = o
        if c == 0:
            near = jnp.where(z + 1 < planes, 1, 0) + jnp.where(z > 0, 1, 0)
            pl.semaphore_wait(barrier, (G - 1) + (n_tp - 1) + near)
        scan_start(0, c)

    def kv_lanes(r):
        return pl.ds(pl.multiple_of((r * kv_heads // G) * HD, HD), HD)

    def soft_copies(which):
        out = []
        for d in range(1, G):
            r = member(d)
            rows = pl.ds(pl.multiple_of(p * length, length), length)
            refs = (
                (sk.at[:, kv_lanes(r)], kv.at[z, 0, rows]),
                (sv.at[:, kv_lanes(r)], kv.at[z, 1, rows]),
                (doc, doc_in.at[p]),
                (sq.at[:, pl.ds(pl.multiple_of(r * qw, HD), qw)], q_in.at[p]),
            )
            for i in which:
                src, dst = refs[i]
                out.append(
                    remote(src, dst, s_send.at[d - 1, i], s_recv.at[d - 1, i], at_member(r))
                )
        return out

    for load in loads[2:6]:
        load.wait()
    own_rows = pl.ds(pl.multiple_of(p * length, length), length)
    kv[z, 0, own_rows] = sk[:, kv_lanes(p)]
    kv[z, 1, own_rows] = sv[:, kv_lanes(p)]
    doc_in[p] = doc[...]
    q_in[p] = sq[:, pl.ds(pl.multiple_of(p * qw, HD), qw)]

    lower = lax.broadcasted_iota(jnp.int32, (length, length), 0) >= lax.broadcasted_iota(
        jnp.int32, (length, length), 1
    )

    def intra_forward(hs):
        qs = [lq[:, lanes(h)] for h in hs]
        ks = [lk[:, lanes(h)] for h in hs]
        vs = [lv[:, lanes(h)] for h in hs]
        ws = [jnp.where(lower, dot(a, b, 1, 1), 0.0).astype(bf16) for a, b in zip(qs, ks)]
        ms = [dot(w, v, 1, 0) for w, v in zip(ws, vs)]
        for h, w, m in zip(hs, ws, ms):
            scores[h] = w
            mix[:, lanes(h)] = m

    for copy in soft_copies((0, 1, 2)):
        copy.start()
    for c in range(hq):
        intra_forward(chunk_heads(c))

    def kv_hop(k):
        block = kv.at[z - k + 1]
        return remote(block, block, kvz_send.at[k - 1], kvz_recv.at[k - 1], at_plane(z + 1))

    def kv_arrival(k):
        block = kv.at[z - k]
        return remote(block, block, kvz_send.at[k - 1], kvz_recv.at[k - 1], at_plane(z - 1))

    def hops(k):
        return (z + 1 < planes) & (z - k + 1 >= 0)

    def kv_pass(k):
        @pl.when(hops(k))
        def _():
            if k > 1:
                kv_arrival(k - 1).wait_recv()
            kv_hop(k).start()

    span = G * length
    factor = math.log2(math.e) / math.sqrt(HD)

    def tile(b, zz, first, count):
        keys = kv[zz, 0, :count]
        vals = kv[zz, 1, :count]
        raw = dot(keys, q_rows[...], 1, 1) * factor
        row = lax.broadcasted_iota(jnp.int32, (count, qw), 0)
        begins = jnp.concatenate([doc_in[b][0:1, :]] * mine, axis=1)
        allowed = row >= begins - zz * span
        if first:
            one = lax.broadcasted_iota(jnp.int32, (1, length), 1)
            allowed = allowed & (row <= b * length + jnp.concatenate([one] * mine, axis=1))
        raw = jnp.where(allowed, raw, floor_score)
        high = jnp.max(raw, axis=0, keepdims=True)
        if not first:
            old = top[...]
            high = jnp.maximum(old, high)
            shrink = jnp.exp2(old - high)
        probs = jnp.exp2(raw - high)
        summed = jnp.sum(probs, axis=0, keepdims=True)
        update = dot(vals, probs.astype(bf16), 0, 0)
        top[...] = high
        if first:
            total[...] = summed
            acc[...] = update
        else:
            total[...] = total[...] * shrink + summed
            acc[...] = acc[...] * shrink + update

    def out_copy(b, d):
        return remote(
            o_own.at[b], soft_out.at[:, pl.ds(pl.multiple_of(p * qw, HD), qw)],
            o_send.at[d], o_recv.at[d], at_member(b),
        )

    def query_block(i, _):
        b = member(i + 1)
        for h in range(mine):
            q_rows[h * length : (h + 1) * length, :] = q_in[b, :, h * HD : (h + 1) * HD]

        @pl.when(b < G // 2)
        def _():
            tile(b, z, True, span // 2)

        @pl.when(b >= G // 2)
        def _():
            tile(b, z, True, span)

        def earlier_plane(k, _):
            @pl.when((i == 0) & jnp.logical_not(hops(k + 1)))
            def _():
                kv_arrival(k).wait_recv()

            tile(b, z - k, False, span)
            return 0

        lax.fori_loop(1, z + 1, earlier_plane, 0)
        out = acc[...] / total[...]
        for h in range(mine):
            o_own[b, :, h * HD : (h + 1) * HD] = jnp.transpose(
                out[:, h * length : (h + 1) * length]
            ).astype(bf16)

        @pl.when(i < G - 1)
        def _():
            out_copy(b, i).start()

        return 0

    for c in range(hq):
        scan_middle(0, c)
        scan_end(0, c)
    for copy in soft_copies((3,)):
        copy.start()
    for copy in soft_copies((0, 1, 2)):
        copy.wait_recv()
    kv_pass(1)
    loads[6].wait()

    ex_own[...] = jnp.zeros_like(ex_own)

    def inter_forward(hs):
        qs = [lq[:, lanes(h)] for h in hs]
        ss = [st_fin[0, h] for h in hs]
        ms = [mix[:, lanes(h)] + dot(a, s, 1, 0) for h, a, s in zip(hs, qs, ss)]
        gs = [lg[:, lanes(h)].astype(f32) for h in hs]
        square, inner = ex_own[0], ex_own[1]
        for m, g in zip(ms, gs):
            square = square + m * m
            inner = inner + g * m
        ex_own[0] = square
        ex_own[1] = inner
        for h, m in zip(hs, ms):
            mix[:, lanes(h)] = m

    for c in range(hq):
        scan_done(0, c)
        inter_forward(chunk_heads(c))

    def exchange():
        return [
            remote(
                ex_own, ex_in.at[k - 1], e_send.at[k - 1], e_recv.at[k - 1],
                {"tp": lax.rem(tp + k, n_tp)},
            )
            for k in range(1, n_tp)
        ]

    for copy in exchange():
        copy.start()
    if planes > 2:
        kv_pass(2)
    for copy in exchange():
        copy.wait_recv()
    square, inner = ex_own[0], ex_own[1]
    for k in range(n_tp - 1):
        square = square + ex_in[k, 0]
        inner = inner + ex_in[k, 1]
    features = heads * HD * n_tp
    scale = lax.rsqrt(jnp.sum(square, axis=1, keepdims=True) / features + epsilon)
    mean = scale * jnp.sum(inner, axis=1, keepdims=True) / features

    def turn(hs):
        qs = [lq[:, lanes(h)] for h in hs]
        ns = [mix[:, lanes(h)] * scale for h in hs]
        gs = [(scale * (lg[:, lanes(h)].astype(f32) - m * mean)).astype(bf16) for h, m in zip(hs, ns)]
        adj = [dot(a, g, 0, 0).astype(bf16) for a, g in zip(qs, gs)]
        for h, m, g, o in zip(hs, ns, gs, adj):
            lin_out[:, lanes(h)] = m.astype(bf16)
            gmix[:, lanes(h)] = g
            st_own[1, h] = o

    for c in range(hq):
        turn(chunk_heads(c))
        scan_start(1, c)
    for k in range(3, planes):
        kv_pass(k)

    def intra_backward(hs):
        qs = [lq[:, lanes(h)] for h in hs]
        ks = [lk[:, lanes(h)] for h in hs]
        vs = [lv[:, lanes(h)] for h in hs]
        gs = [gmix[:, lanes(h)] for h in hs]
        ss = [st_fin[0, h] for h in hs]
        ws = [scores[h] for h in hs]
        ds = [jnp.where(lower, dot(g, v, 1, 1), 0.0).astype(bf16) for g, v in zip(gs, vs)]
        gq = [dot(d, k, 1, 0) + dot(g, s, 1, 1) for d, k, g, s in zip(ds, ks, gs, ss)]
        gk = [dot(d, q, 0, 0) for d, q in zip(ds, qs)]
        gv = [dot(w, g, 0, 0) for w, g in zip(ws, gs)]
        for h, a, b, c in zip(hs, gq, gk, gv):
            grad_q[:, lanes(h)] = a.astype(bf16)
            gk_acc[:, lanes(h)] = b
            gv_acc[:, lanes(h)] = c

    for c in range(hq):
        intra_backward(chunk_heads(c))
        scan_middle(1, c)

    for copy in soft_copies((3,)):
        copy.wait_recv()
    ahead = jnp.where(z == 0, G, jnp.where(z < planes // 2, G // 2, 0))
    lax.fori_loop(0, ahead, query_block, 0)
    for c in range(hq):
        scan_end(1, c)
    lax.fori_loop(ahead, G, query_block, 0)
    soft_out[:, pl.ds(pl.multiple_of(p * qw, HD), qw)] = o_own[p]

    def inter_backward(hs):
        ks = [lk[:, lanes(h)] for h in hs]
        vs = [lv[:, lanes(h)] for h in hs]
        ss = [st_fin[1, h] for h in hs]
        gk = [gk_acc[:, lanes(h)] + dot(v, s, 1, 1) for h, v, s in zip(hs, vs, ss)]
        gv = [gv_acc[:, lanes(h)] + dot(k, s, 1, 0) for h, k, s in zip(hs, ks, ss)]
        for h, a, b in zip(hs, gk, gv):
            grad_k[:, lanes(h)] = a.astype(bf16)
            grad_v[:, lanes(h)] = b.astype(bf16)

    for c in range(hq):
        scan_done(1, c)
        inter_backward(chunk_heads(c))

    out_copies = [out_copy(member(d + 1), d) for d in range(G - 1)]
    for copy in out_copies:
        copy.wait_recv()
    for way in (0, 1):
        for c in range(hq):
            for copy in scan_a(way, c) + scan_c(way, c):
                copy.wait_send()
    for copy in soft_copies((0, 1, 2, 3)) + exchange() + out_copies:
        copy.wait_send()
    for k in range(1, planes):

        @pl.when(hops(k))
        def _():
            kv_hop(k).wait_send()

    for way in (0, 1):

        @pl.when(passes_on(way))
        def _():
            for c in range(hq):
                scan_z(way, c).wait_send()


def on_device(n, n_tp, lq, lk, lv, lg, sq, sk, sv, doc_start):
    length, width = lq.shape
    heads = width // HD
    hq = heads // G
    planes = n // G
    q_width = sq.shape[1]
    qw = q_width // G
    doc_row = doc_start.reshape(1, length)
    dma = pltpu.SemaphoreType.DMA
    vm = pltpu.VMEM
    span = G * length
    others = planes - 1
    kv_width = sk.shape[1]
    scratch = [
        vm((length, width), bf16), vm((length, width), bf16),
        vm((length, width), bf16), vm((length, width), bf16),
        vm((length, q_width), bf16), vm((length, kv_width), bf16), vm((length, kv_width), bf16),
        vm((8, length), jnp.int32),
        dma((7,)),
        vm((2, heads, HD, HD), bf16),
        vm((2, G, hq, HD, HD), bf16),
        vm((2, hq, HD, HD), bf16),
        vm((2, hq, HD, HD), bf16),
        vm((2, G, hq, HD, HD), bf16),
        vm((2, heads, HD, HD), bf16),
        vm((heads, length, length), bf16),
        vm((length, width), f32),
        vm((length, width), bf16),
        vm((length, width), f32),
        vm((length, width), f32),
        vm((2, length, HD), f32),
        vm((n_tp - 1, 2, length, HD), f32),
        vm((planes, 2, span, HD), bf16),
        vm((G, length, qw), bf16),
        vm((qw // HD * length, HD), bf16),
        vm((G, 8, length), jnp.int32),
        vm((G, length, qw), bf16),
        vm((1, qw), f32),
        vm((1, qw), f32),
        vm((HD, qw), f32),
        vm((HD, HD), f32),
        vm((hq, HD, HD), f32),
        dma((2, G - 1, hq)), dma((2, G - 1, hq)),
        dma((2, hq)), dma((2, hq)),
        dma((2, G - 1, hq)), dma((2, G - 1, hq)),
        dma((n_tp - 1,)), dma((n_tp - 1,)),
        dma((G - 1, 4)), dma((G - 1, 4)),
        dma((others,)), dma((others,)),
        dma((G - 1,)), dma((G - 1,)),
    ]
    hbm = pl.BlockSpec(memory_space=pl.ANY)
    here = pl.BlockSpec(memory_space=pltpu.VMEM)
    widths = [width] * 4 + [q_width]
    held = pl.pallas_call(
        functools.partial(kernel, n, n_tp),
        out_shape=[pltpu.VMEM((length, w), bf16) for w in widths],
        in_specs=[hbm] * 7 + [here],
        out_specs=[here] * 5,
        scratch_shapes=scratch,
        compiler_params=pltpu.CompilerParams(
            collective_id=0, has_side_effects=True, vmem_limit_bytes=52 * 1024 * 1024
        ),
    )(lq, lk, lv, lg, sq, sk, sv, doc_row)
    return pl.pallas_call(
        write_out,
        out_shape=[jax.ShapeDtypeStruct((length, w), bf16) for w in widths],
        in_specs=[here] * 5,
        out_specs=[hbm] * 5,
        scratch_shapes=[dma((5,))],
        compiler_params=pltpu.CompilerParams(vmem_limit_bytes=8 * 1024 * 1024),
    )(*held)


def write_out(*refs):
    sems = refs[10]
    copies = [pltpu.make_async_copy(refs[i], refs[5 + i], sems.at[i]) for i in range(5)]
    for copy in copies:
        copy.start()
    for copy in copies:
        copy.wait()


def solution(mesh):
    wide = P("ctx", "tp")
    return jax.shard_map(
        functools.partial(on_device, mesh.shape["ctx"], mesh.shape["tp"]),
        mesh=mesh,
        in_specs=(wide,) * 7 + (P("ctx"),),
        out_specs=(wide,) * 5,
        check_vma=False,
    )
```
